32 devices in a mesh: elem: 8 (over z, x), blk: 4 (over y, core).
Axes of the slice: x: 2, y: 2, z: 4, core: 2. Of those that a mesh axis runs over, the one named last changes fastest.
Arguments:
- basis: bfloat16 [4096, 3, 512], P('elem'), may hold values from -6 to 6
- send_rows: int32 [8, 4, 256], P('elem', 'blk'), may hold values from 0 to 511
- elem_slot: int32 [8, 2048], P(None, ('elem', 'blk')), may hold values from 0 to 255, as said below
- set_size: int32 [8], replicated, may hold values from 1 to 256, 1280 in all
- elem_weight: float32 [2048], P(('elem', 'blk')), may hold values from 0.2 to 5
- element_stiffening: float32 [2048], P(('elem', 'blk')), may hold values from 1 to 8
- state: bfloat16 [512], replicated, may hold values from -0.25 to 0.25
- load: float32 [512], P('blk'), may hold values from -6 to 6
Outputs:
- tangent: float32 [512, 512], P('elem', 'blk')
- residual: float32 [512], P('blk')
The draws below stay inside these ranges and needn't reach their ends.
Inputs may be any that keep to these rules, and one draw needn't show every extreme that they name: `elem_slot`: for element column of device (s, b): p names slot p % 32 of what owner p // 32 sends to that device. From each owner only its first n slots are named, n at most 32; for every device exactly one owner gives 32, and the n over all owners sum to 128.
All inputs are finite; a program needn't handle non-finite values.
Results may differ from the reference program's by a relative error of at most 0.0003.
Values may be sent and summed in bfloat16 or wider, within the bound.
A program may use at most 64 MiB of HBM per device.

```python
import math
import jax
import jax.numpy as jnp
import numpy as np
from jax import lax

MODE_COUNT = 512
ELEMENT_SLOTS = 64
SETS = 8
SET_ELEMS = 256
ELEMS = 2048
NODES_DEV = 512
NODES = 4096
CAP = 32
LIVE = 1280
N_BLK = 4


def draw_elem_slot(key, part):
    units = SETS * N_BLK
    used = 2 * ELEMENT_SLOTS
    heavy_key, order_key, pick_key = jax.random.split(key, 3)
    source = lax.broadcasted_iota(jnp.int32, (units, SETS), 1)
    heavy = jax.random.randint(heavy_key, (units, 1), 0, SETS)
    scores = jax.random.randint(order_key, (units, SETS), 0, 1 << 20) * SETS + source
    scores = jnp.where(source == heavy, (1 << 20) * SETS + source, scores)
    rank = jnp.argsort(jnp.argsort(scores, axis=1), axis=1)
    base = (used - CAP) // (SETS - 1)
    extra = used - CAP - base * (SETS - 1)
    counts = jnp.where(source == heavy, CAP, base + (rank < extra).astype(jnp.int32))
    ends = jnp.cumsum(counts, axis=1)
    starts = ends - counts
    pick = jax.random.randint(pick_key, (units, 8 * ELEMENT_SLOTS), 0, used)
    owner = jnp.sum((ends[:, None, :] <= pick[:, :, None]).astype(jnp.int32), axis=2)
    first = jnp.take_along_axis(starts, owner, axis=1)
    slot = owner * CAP + pick - first
    return slot.reshape(units, ELEMENT_SLOTS, 8).transpose(2, 0, 1).reshape(8, units * ELEMENT_SLOTS).astype(jnp.int32)


def with_ends(values, stream_key, least, top_value):
    place = [jax.random.randint(jax.random.fold_in(stream_key, axis), (), 0, length) for axis, length in enumerate(values.shape)]
    widest = values.shape.index(max(values.shape))
    beside = place[:widest] + [(place[widest] + 1) % values.shape[widest]] + place[widest + 1:]
    return values.at[tuple(place)].set(least).at[tuple(beside)].set(top_value)


def block_levels(key, extent, shards, smallest, high):
    loudness, own = 1.0, jax.random.fold_in(key, 6)
    for dim, blocks in shards:
        draws = jnp.exp(jax.random.uniform(jax.random.fold_in(own, dim), (blocks,), jnp.float32, smallest / len(shards), high / len(shards)))
        loudness = loudness * jnp.repeat(draws, extent[dim] // blocks).reshape([-1 if axis == dim else 1 for axis in range(len(extent))])
    return loudness


def split_up(number_of, total, bound, lean):
    loads = [(1 << 20) // math.isqrt(standing ** lean) + 1 for standing in range(2, number_of + 1)]
    rest, given = total - bound - (number_of - 1), [1] * (number_of - 1)
    while rest > 0:
        free = [i for i in range(number_of - 1) if given[i] < bound]
        mass, remaining = sum([loads[i] for i in free]), rest
        for i in free:
            addition = min(bound - given[i], max(1, remaining * loads[i] // mass), rest)
            given[i] = given[i] + addition
            rest = rest - addition
    return np.array([bound] + given)


def ragged_sizes(own_key, number_of, total, bound, lean):
    if number_of == 2:
        one = jax.random.randint(own_key, (), max(1, total - bound), min(bound, total - 1) + 1)
        return jnp.stack([one, total - one])
    sizes = jnp.asarray(split_up(number_of, total, bound, lean), jnp.int32)
    pairs = (number_of - 1) // 2
    donor, taker = sizes[1:1 + 2 * pairs:2], sizes[2:2 + 2 * pairs:2]
    slack = jnp.minimum(donor - 1, bound - taker)
    moved = jax.random.randint(jax.random.fold_in(own_key, 1), (pairs,), 0, 1 << 20) % (slack + 1)
    sizes = sizes.at[1:1 + 2 * pairs:2].set(donor - moved).at[2:2 + 2 * pairs:2].set(taker + moved)
    return sizes[jax.random.permutation(jax.random.fold_in(own_key, 2), number_of)]


def gaussian(stream_key, shape, spread, most, cuts=(), held_as=jnp.bfloat16):
    level = block_levels(stream_key, shape, cuts, -0.22, 0.18) if cuts else 1.0
    array = jax.random.normal(stream_key, shape, jnp.float32) * spread * level
    return jnp.minimum(jnp.maximum(array, -most), most).astype(held_as)


def setup_inputs(seed: int = 0) -> dict:
    key_of = jax.random.split(jax.random.key(seed), 9)
    return {
        "basis": gaussian(key_of[0], (NODES, 3, MODE_COUNT), 1.0, 6.0, ((0, 8),)),
        "send_rows": with_ends(jax.random.randint(key_of[1], (SETS, N_BLK, SETS * CAP), 0, NODES_DEV), jax.random.fold_in(key_of[1], 1), 0, NODES_DEV - 1).astype(jnp.int32),
        "elem_slot": draw_elem_slot(jax.random.fold_in(key_of[8], 71), 0),
        "set_size": ragged_sizes(key_of[3], SETS, LIVE, SET_ELEMS, 2).astype(jnp.int32),
        "elem_weight": jnp.clip(jnp.exp(math.log(5.0) - 3.218876 * jax.random.uniform(key_of[4], (ELEMS,), jnp.float32) ** block_levels(key_of[4], (ELEMS,), ((0, 32),), -0.2, 0.2)), 0.2, 5.0),
        "element_stiffening": jnp.clip(jnp.exp(math.log(8.0) - 2.0794415 * jax.random.uniform(key_of[5], (ELEMS,), jnp.float32) ** block_levels(key_of[5], (ELEMS,), ((0, 32),), -0.2, 0.2)), 1.0, 8.0),
        "state": gaussian(key_of[6], (MODE_COUNT,), (0.4 / MODE_COUNT ** 0.5), 0.25),
        "load": gaussian(key_of[7], (MODE_COUNT,), 1.0, 6.0, ((0, 4),), jnp.float32),
    }


def corner_grads():
    corner = jnp.arange(8)[:, None]
    bit = corner // 2 ** jnp.arange(3)[None, :] % 2
    return (bit * 2 - 1).astype(jnp.float32) * 0.25

def element_contributions(basis_matrix, displacement, stiffening_power):
    grads = corner_grads()
    element_count = basis_matrix.shape[0]
    basis_modes = basis_matrix.shape[2]
    corner_nodes = basis_matrix.reshape(element_count, 8, 3, basis_modes)
    grad_basis = jnp.einsum('ak,eacm->ekcm', grads, corner_nodes, precision=lax.Precision.HIGHEST)
    moved = displacement.reshape(8, 3, element_count)
    hgrad = jnp.einsum('ak,ace->kce', grads, moved, precision=lax.Precision.HIGHEST)
    volume = hgrad[0, 0] + hgrad[1, 1] + hgrad[2, 2]
    stiff = 1.0 + stiffening_power * volume ** 2 - 2.0 / 3.0
    press = volume + stiffening_power * volume ** 3 / 3.0 - 2.0 / 3.0 * volume
    eye = jnp.eye(3, dtype=jnp.float32)
    stress = hgrad + jnp.transpose(hgrad, (1, 0, 2)) + press[None, None, :] * eye[:, :, None]
    force_vector = jnp.einsum('ak,kce->ace', grads, stress, precision=lax.Precision.HIGHEST).reshape(24, element_count) + 0.25 * displacement
    sym = grad_basis + jnp.transpose(grad_basis, (0, 2, 1, 3))
    trace_basis = grad_basis[:, 0, 0] + grad_basis[:, 1, 1] + grad_basis[:, 2, 2]
    mode_image = jnp.einsum('ak,ekcm->eacm', grads, sym, precision=lax.Precision.HIGHEST)
    mode_image = mode_image + stiff[:, None, None, None] * grads[None, :, :, None] * trace_basis[:, None, None, :] + 0.25 * corner_nodes
    return (mode_image.reshape(element_count, 24, basis_modes), force_vector)

def reference(basis, send_rows, elem_slot, set_size, elem_weight, element_stiffening, state, load):
    units = SETS * N_BLK
    full_state = state.astype(jnp.float32)

    def step(carry, unit):
        total_tangent, total_force = carry
        group = unit // N_BLK
        block = unit % N_BLK
        slots = lax.dynamic_slice_in_dim(elem_slot, unit * ELEMENT_SLOTS, ELEMENT_SLOTS, 1)
        source = slots // CAP
        local = send_rows[source, block, group * CAP + slots % CAP]
        node_index = source * NODES_DEV + local
        basis_matrix = basis[node_index.T].reshape(ELEMENT_SLOTS, 24, MODE_COUNT).astype(jnp.float32)
        position = block * ELEMENT_SLOTS + jnp.arange(ELEMENT_SLOTS).astype(jnp.int32)
        weights = lax.dynamic_slice_in_dim(elem_weight, unit * ELEMENT_SLOTS, ELEMENT_SLOTS, 0)
        weights = jnp.where(position < set_size[group], weights, jnp.zeros_like(weights))
        stiffening_power = lax.dynamic_slice_in_dim(element_stiffening, unit * ELEMENT_SLOTS, ELEMENT_SLOTS, 0)
        displacement = jnp.einsum('agd,d->ga', basis_matrix, full_state, precision=lax.Precision.HIGHEST)
        mode_image, force_vector = element_contributions(basis_matrix, displacement, stiffening_power)
        weighted_image = lax.optimization_barrier((weights[:, None, None] * mode_image).astype(jnp.bfloat16)).astype(jnp.float32)
        weighted_force = lax.optimization_barrier((force_vector * weights[None, :]).astype(jnp.bfloat16)).astype(jnp.float32)
        partial_tangent = lax.dot_general(basis_matrix, weighted_image, (((0, 1), (0, 1)), ((), ())), precision=lax.Precision.HIGHEST)
        partial_force = lax.dot_general(basis_matrix, weighted_force, (((0, 1), (1, 0)), ((), ())), precision=lax.Precision.HIGHEST)
        return ((total_tangent + partial_tangent, total_force + partial_force), None)
    start = (jnp.zeros((MODE_COUNT, MODE_COUNT), jnp.float32), jnp.zeros((MODE_COUNT,), jnp.float32))
    (tangent, force_vector), _ = lax.scan(step, start, jnp.arange(units).astype(jnp.int32))
    scale = lax.rsqrt(24.0 * jnp.sum(set_size).astype(jnp.float32))
    return (tangent * scale, force_vector * scale - load)
```

```python
import functools

import jax
import jax.numpy as jnp
from jax import lax
from jax.experimental import pallas as pl
from jax.experimental.pallas import tpu as pltpu
from jax.sharding import PartitionSpec as P

LANES = 128
MESH = pl.DeviceIdType.MESH


def corner_grads():
    corner = jnp.arange(8)[:, None]
    bit = corner // 2 ** jnp.arange(3)[None, :] % 2
    return (bit * 2 - 1).astype(jnp.float32) * 0.25


def element_contributions(basis_matrix, displacement, stiffening_power):
    grads = corner_grads()
    element_count = basis_matrix.shape[0]
    basis_modes = basis_matrix.shape[2]
    corner_nodes = basis_matrix.reshape(element_count, 8, 3, basis_modes)
    grad_basis = jnp.einsum(
        "ak,eacm->ekcm",
        grads.astype(jnp.bfloat16),
        corner_nodes,
        preferred_element_type=jnp.float32,
    )
    moved = displacement.reshape(8, 3, element_count)
    hgrad = jnp.einsum("ak,ace->kce", grads, moved, precision=lax.Precision.HIGHEST)
    volume = hgrad[0, 0] + hgrad[1, 1] + hgrad[2, 2]
    stiff = 1.0 + stiffening_power * volume**2 - 2.0 / 3.0
    press = volume + stiffening_power * volume**3 / 3.0 - 2.0 / 3.0 * volume
    eye = jnp.eye(3, dtype=jnp.float32)
    stress = hgrad + jnp.transpose(hgrad, (1, 0, 2)) + press[None, None, :] * eye[:, :, None]
    force_vector = (
        jnp.einsum("ak,kce->ace", grads, stress, precision=lax.Precision.HIGHEST).reshape(
            24, element_count
        )
        + 0.25 * displacement
    )
    sym = grad_basis + jnp.transpose(grad_basis, (0, 2, 1, 3))
    trace_basis = grad_basis[:, 0, 0] + grad_basis[:, 1, 1] + grad_basis[:, 2, 2]
    mode_image = jnp.einsum("ak,ekcm->eacm", grads, sym, precision=lax.Precision.HIGHEST)
    mode_image = (
        mode_image
        + stiff[:, None, None, None] * grads[None, :, :, None] * trace_basis[:, None, None, :]
        + 0.25 * corner_nodes.astype(jnp.float32)
    )
    return (mode_image.reshape(element_count, 24, basis_modes), force_vector)


def local(basis, send_rows, elem_slot, set_size, elem_weight, element_stiffening, state, load):
    nodes = basis.shape[0]
    basis_modes = basis.shape[2]
    flat = basis.reshape(nodes, 3 * basis_modes)
    outgoing = jnp.take(flat, send_rows[0, 0], axis=0)
    arrived = lax.all_to_all(outgoing, "elem", split_axis=0, concat_axis=0, tiled=True)
    element_count = elem_slot.shape[1]
    chosen_elements = jnp.take(arrived, elem_slot.T.reshape(-1), axis=0)
    basis_matrix = chosen_elements.reshape(element_count, 24, basis_modes)
    set_index = lax.axis_index("elem")
    block_index = lax.axis_index("blk")
    live = lax.dynamic_index_in_dim(set_size, set_index, keepdims=False)
    position = block_index * element_count + jnp.arange(element_count, dtype=jnp.int32)
    weights = jnp.where(position < live, elem_weight, jnp.zeros_like(elem_weight))
    displacement = jnp.einsum("agd,d->ga", basis_matrix, state, preferred_element_type=jnp.float32)
    mode_image, force_vector = element_contributions(basis_matrix, displacement, element_stiffening)
    weighted_image = (weights[:, None, None] * mode_image).astype(jnp.bfloat16)
    weighted_force = (force_vector * weights[None, :]).astype(jnp.bfloat16)
    tangent = lax.dot_general(
        basis_matrix,
        weighted_image,
        (((0, 1), (0, 1)), ((), ())),
        preferred_element_type=jnp.float32,
    )
    force_all = lax.dot_general(
        basis_matrix,
        weighted_force,
        (((0, 1), (1, 0)), ((), ())),
        preferred_element_type=jnp.float32,
    )
    halfway, force_part = (
        lax.psum_scatter(tangent, "blk", scatter_dimension=1, tiled=True),
        lax.psum_scatter(force_all, "blk", scatter_dimension=0, tiled=True),
    )
    mine = lax.psum_scatter(halfway, "elem", scatter_dimension=0, tiled=True)
    force_cols = lax.psum(force_part, "elem")
    scale = lax.rsqrt(24.0 * jnp.sum(set_size).astype(jnp.float32))
    return (mine * scale, force_cols * scale - load)


def signs(corner):
    return [1.0 if corner >> axis & 1 else -1.0 for axis in range(3)]


def signed_sum(terms, sign):
    total = terms[0] if sign[0] > 0 else -terms[0]
    for term, one in zip(terms[1:], sign[1:]):
        total = total + term if one > 0 else total - term
    return total


def fused_kernel(
    devs,
    basis_ref,
    send_ref,
    slot_ref,
    size_ref,
    aux_ref,
    state_ref,
    load_ref,
    tangent_ref,
    residual_ref,
    out_rows,
    arr,
    v_ref,
    vt_ref,
    w_ref,
    g_ref,
    part,
    recv_core,
    mid,
    recv_first,
    recv_second,
    acc,
    recv_z,
    gather_send,
    gather_recv,
    core_send,
    core_recv,
    first_send,
    first_recv,
    second_send,
    second_recv,
    z_send,
    z_recv,
):
    nodes = basis_ref.shape[1]
    modes = basis_ref.shape[2]
    slots = arr.shape[1]
    cap = slots // devs
    elements = aux_ref.shape[1] // 2
    corners = 8 * elements
    planes = devs // 2
    rows = modes // devs
    me = lax.axis_index("elem")
    blk = lax.axis_index("blk")
    x, z = lax.rem(me, 2), me // 2
    core, y = lax.rem(blk, 2), blk // 2
    core_peer = (me, y * 2 + 1 - core)
    y_peer = (me, (1 - y) * 2 + core)
    x_peer = (z * 2 + 1 - x, blk)

    barrier = pltpu.get_barrier_semaphore()
    for step in range(1, devs):
        pl.semaphore_signal(
            barrier, inc=1, device_id=(lax.rem(me + step, devs), blk), device_id_type=MESH
        )
    for peer in (core_peer, y_peer):
        pl.semaphore_signal(barrier, inc=1, device_id=peer, device_id_type=MESH)

    asked = jnp.broadcast_to(send_ref[...], (nodes, slots))
    pick_t = jnp.where(lax.broadcasted_iota(jnp.int32, (nodes, slots), 0) == asked, 1.0, 0.0)
    pick = jnp.transpose(pick_t).astype(jnp.bfloat16)
    for c in range(3):
        out_rows[c] = jnp.dot(
            pick, basis_ref[c], preferred_element_type=jnp.float32
        ).astype(jnp.bfloat16)

    pl.semaphore_wait(barrier, devs + 1)
    mine = pl.ds(pl.multiple_of(me * cap, cap), cap)
    copies = []
    for step in range(1, devs):
        dest = lax.rem(me + step, devs)
        copy = pltpu.make_async_remote_copy(
            src_ref=out_rows.at[:, pl.ds(pl.multiple_of(dest * cap, cap), cap), :],
            dst_ref=arr.at[:, mine, :],
            send_sem=gather_send.at[step - 1],
            recv_sem=gather_recv.at[step - 1],
            device_id=(dest, blk),
            device_id_type=MESH,
        )
        copy.start()
        copies.append(copy)
    arr[:, mine, :] = out_rows[:, mine, :]

    wanted = jnp.broadcast_to(slot_ref[...], (slots, corners))
    spread_t = jnp.where(lax.broadcasted_iota(jnp.int32, (slots, corners), 0) == wanted, 1.0, 0.0)
    spread = jnp.transpose(spread_t)
    spread_t = spread_t.astype(jnp.bfloat16)
    by_corner = [spread[a * elements : (a + 1) * elements] for a in range(8)]
    coef = jnp.concatenate(
        [0.25 * signed_sum(by_corner, [signs(a)[k] for a in range(8)]) for k in range(3)], axis=0
    ).astype(jnp.bfloat16)
    spread = spread.astype(jnp.bfloat16)
    columns = jnp.transpose(jnp.broadcast_to(aux_ref[...], (LANES, 2 * elements)))
    live = size_ref[me]
    position = blk * elements + lax.broadcasted_iota(jnp.int32, (elements, LANES), 0)
    omega = jnp.where(position < live, columns[:elements], 0.0)
    stiffening = columns[elements:]
    state_rows = jnp.broadcast_to(state_ref[...].astype(jnp.float32), (LANES, modes)).astype(
        jnp.bfloat16
    )
    for copy in copies:
        copy.wait()

    disp = []
    for c in range(3):
        rows_c = arr[c]
        v = jnp.dot(spread, rows_c, preferred_element_type=jnp.float32).astype(jnp.bfloat16)
        v_ref[c] = v
        vt_ref[c] = lax.dot_general(
            rows_c, spread_t, (((0,), (0,)), ((), ())), preferred_element_type=jnp.float32
        ).astype(jnp.bfloat16)
        g_ref[c] = jnp.dot(coef, rows_c, preferred_element_type=jnp.float32)
        moved = lax.dot_general(
            v, state_rows, (((1,), (1,)), ((), ())), preferred_element_type=jnp.float32
        )
        disp.append([moved[a * elements : (a + 1) * elements] for a in range(8)])

    hgrad = [
        [0.25 * signed_sum(disp[c], [signs(a)[k] for a in range(8)]) for c in range(3)]
        for k in range(3)
    ]
    volume = hgrad[0][0] + hgrad[1][1] + hgrad[2][2]
    square = stiffening * volume * volume
    lam = 1.0 + square - 2.0 / 3.0
    press = volume + square * volume / 3.0 - 2.0 / 3.0 * volume
    quarter = 0.25 * omega

    force = jnp.zeros((LANES, modes), jnp.float32)
    for c in range(3):
        stress = [
            hgrad[k][c] + hgrad[c][k] + press if k == c else hgrad[k][c] + hgrad[c][k]
            for k in range(3)
        ]
        wforce = jnp.concatenate(
            [quarter * (signed_sum(stress, signs(a)) + disp[c][a]) for a in range(8)], axis=0
        ).astype(jnp.bfloat16)
        force = force + lax.dot_general(
            wforce, v_ref[c], (((0,), (0,)), ((), ())), preferred_element_type=jnp.float32
        )

    for q in range(modes // LANES):
        lanes = pl.ds(q * LANES, LANES)
        grad = [
            [g_ref[c, pl.ds(k * elements, elements), lanes] for c in range(3)] for k in range(3)
        ]
        trace = lam * (grad[0][0] + grad[1][1] + grad[2][2])
        for c in range(3):
            terms = [
                quarter * (grad[k][c] + grad[c][k] + trace if k == c else grad[k][c] + grad[c][k])
                for k in range(3)
            ]
            for a in range(4):
                half = signed_sum(terms, signs(a))
                for corner, image in ((a, half), (7 - a, -half)):
                    at = pl.ds(corner * elements, elements)
                    w_ref[c, at, lanes] = (
                        image + quarter * v_ref[c, at, lanes].astype(jnp.float32)
                    ).astype(jnp.bfloat16)

    for q in range(modes // LANES):
        lanes = pl.ds(q * LANES, LANES)
        to_y, to_core = q // 2, q % 2
        block = jnp.dot(vt_ref[0], w_ref[0, :, lanes], preferred_element_type=jnp.float32)
        for c in (1, 2):
            block = block + jnp.dot(
                vt_ref[c], w_ref[c, :, lanes], preferred_element_type=jnp.float32
            )
        tail = force[:8, q * LANES : (q + 1) * LANES]
        for dest in range(devs):
            to_x, to_z = dest % 2, dest // 2
            p, zz = to_z // (planes // 2), to_z % (planes // 2)
            f, s = (to_y, to_x) if p == 0 else (to_x, to_y)
            part[p, to_core, f, s, zz, :rows] = block[dest * rows : (dest + 1) * rows]
            part[p, to_core, f, s, zz, rows:] = tail

    cores = []
    for p in range(2):
        copy = pltpu.make_async_remote_copy(
            src_ref=part.at[p, 1 - core],
            dst_ref=recv_core.at[p],
            send_sem=core_send.at[p],
            recv_sem=core_recv.at[p],
            device_id=core_peer,
            device_id_type=MESH,
        )
        copy.start()
        cores.append(copy)
    order = (((y, y_peer), (x, x_peer)), ((x, x_peer), (y, y_peer)))
    firsts = []
    for p in range(2):
        at, peer = order[p][0]
        cores[p].wait_recv()
        mid[p, 1 - at] = part[p, core, 1 - at] + recv_core[p, 1 - at]
        copy = pltpu.make_async_remote_copy(
            src_ref=mid.at[p, 1 - at],
            dst_ref=recv_first.at[p],
            send_sem=first_send.at[p],
            recv_sem=first_recv.at[p],
            device_id=peer,
            device_id_type=MESH,
        )
        copy.start()
        firsts.append(copy)
    seconds = []
    for p in range(2):
        at = order[p][0][0]
        there, peer = order[p][1]
        mid[p, at] = part[p, core, at] + recv_core[p, at]
        firsts[p].wait_recv()
        mid[p, at, 1 - there] = mid[p, at, 1 - there] + recv_first[p, 1 - there]
        copy = pltpu.make_async_remote_copy(
            src_ref=mid.at[p, at, 1 - there],
            dst_ref=recv_second.at[p],
            send_sem=second_send.at[p],
            recv_sem=second_recv.at[p],
            device_id=peer,
            device_id_type=MESH,
        )
        copy.start()
        seconds.append(copy)
    for p in range(2):
        at = order[p][0][0]
        there = order[p][1][0]
        seconds[p].wait_recv()
        acc[pl.ds(p * (planes // 2), planes // 2)] = (
            mid[p, at, there] + recv_first[p, there] + recv_second[p]
        )
    lasts = []
    for step in range(1, planes):
        dest = lax.rem(z + step, planes)
        copy = pltpu.make_async_remote_copy(
            src_ref=acc.at[dest],
            dst_ref=recv_z.at[step - 1],
            send_sem=z_send.at[step - 1],
            recv_sem=z_recv.at[step - 1],
            device_id=(dest * 2 + x, blk),
            device_id_type=MESH,
        )
        copy.start()
        lasts.append(copy)
    count = size_ref[0]
    for i in range(1, devs):
        count = count + size_ref[i]
    scale = lax.rsqrt(jnp.full((8, LANES), 24.0 * count.astype(jnp.float32), jnp.float32))
    total = acc[z]
    for step in range(1, planes):
        lasts[step - 1].wait_recv()
        total = total + recv_z[step - 1]
    tangent_ref[...] = total[:rows] * jnp.tile(scale, (rows // 8, 1))
    residual_ref[...] = (total[rows:] * scale)[:1] - load_ref[...]
    for copy in cores + firsts + seconds + lasts:
        copy.wait_send()


def fused(devs, basis, send_rows, elem_slot, set_size, elem_weight, element_stiffening, state, load):
    nodes, _, modes = basis.shape
    slots = send_rows.shape[2]
    elements = elem_slot.shape[1]
    corners = 8 * elements
    rows = modes // devs
    half = devs // 4
    block = (half, rows + 8, LANES)
    f32, b16 = jnp.float32, jnp.bfloat16
    dma = pltpu.SemaphoreType.DMA
    vmem = pl.BlockSpec(memory_space=pltpu.VMEM)
    smem = pl.BlockSpec(memory_space=pltpu.SMEM)
    tangent, residual = pl.pallas_call(
        functools.partial(fused_kernel, devs),
        out_shape=(
            jax.ShapeDtypeStruct((rows, LANES), f32),
            jax.ShapeDtypeStruct((1, LANES), f32),
        ),
        in_specs=[vmem, vmem, vmem, smem, vmem, vmem, vmem],
        out_specs=(vmem, vmem),
        scratch_shapes=[
            pltpu.VMEM((3, slots, modes), b16),
            pltpu.VMEM((3, slots, modes), b16),
            pltpu.VMEM((3, corners, modes), b16),
            pltpu.VMEM((3, modes, corners), b16),
            pltpu.VMEM((3, corners, modes), b16),
            pltpu.VMEM((3, 3 * elements, modes), f32),
            pltpu.VMEM((2, 2, 2, 2) + block, f32),
            pltpu.VMEM((2, 2, 2) + block, f32),
            pltpu.VMEM((2, 2, 2) + block, f32),
            pltpu.VMEM((2, 2) + block, f32),
            pltpu.VMEM((2,) + block, f32),
            pltpu.VMEM((devs // 2, rows + 8, LANES), f32),
            pltpu.VMEM((devs // 2 - 1, rows + 8, LANES), f32),
            dma((devs - 1,)),
            dma((devs - 1,)),
            dma((2,)),
            dma((2,)),
            dma((2,)),
            dma((2,)),
            dma((2,)),
            dma((2,)),
            dma((devs // 2 - 1,)),
            dma((devs // 2 - 1,)),
        ],
        compiler_params=pltpu.CompilerParams(
            collective_id=0, has_side_effects=True, vmem_limit_bytes=40 * 1024 * 1024
        ),
        cost_estimate=pl.CostEstimate(
            flops=6 * modes * modes * corners, bytes_accessed=2 * basis.size, transcendentals=0
        ),
        name="galerkin",
    )(
        jnp.transpose(basis, (1, 0, 2)),
        send_rows.reshape(1, slots),
        elem_slot.reshape(1, corners),
        set_size,
        jnp.concatenate([elem_weight, element_stiffening]).reshape(1, 2 * elements),
        state.reshape(1, modes),
        load.reshape(1, LANES),
    )
    return tangent, residual.reshape(LANES)


def solution(mesh):
    in_specs = (
        P("elem", None, None),
        P("elem", "blk", None),
        P(None, ("elem", "blk")),
        P(),
        P(("elem", "blk")),
        P(("elem", "blk")),
        P(),
        P("blk"),
    )
    out_specs = (P("elem", "blk"), P("blk"))
    devs, blocks = mesh.shape["elem"], mesh.shape["blk"]

    def run(*args):
        modes, slots, elements = args[0].shape[2], args[1].shape[2], args[2].shape[1] // mesh.size
        fits = (
            blocks == 4
            and modes == blocks * LANES
            and devs % 4 == 0
            and modes % (8 * devs) == 0
            and slots % (16 * devs) == 0
            and 2 * elements == LANES
        )
        part = functools.partial(fused, devs) if fits else local
        return jax.shard_map(
            part, mesh=mesh, in_specs=in_specs, out_specs=out_specs, check_vma=False
        )(*args)

    return run
```

```python
import functools

import jax
import jax.numpy as jnp
from jax import lax
from jax.experimental import pallas as pl
from jax.experimental.pallas import tpu as pltpu
from jax.sharding import PartitionSpec as P

LANES = 128
MESH = pl.DeviceIdType.MESH


def corner_grads():
    corner = jnp.arange(8)[:, None]
    bit = corner // 2 ** jnp.arange(3)[None, :] % 2
    return (bit * 2 - 1).astype(jnp.float32) * 0.25


def element_contributions(basis_matrix, displacement, stiffening_power):
    grads = corner_grads()
    element_count = basis_matrix.shape[0]
    basis_modes = basis_matrix.shape[2]
    corner_nodes = basis_matrix.reshape(element_count, 8, 3, basis_modes)
    grad_basis = jnp.einsum(
        "ak,eacm->ekcm",
        grads.astype(jnp.bfloat16),
        corner_nodes,
        preferred_element_type=jnp.float32,
    )
    moved = displacement.reshape(8, 3, element_count)
    hgrad = jnp.einsum("ak,ace->kce", grads, moved, precision=lax.Precision.HIGHEST)
    volume = hgrad[0, 0] + hgrad[1, 1] + hgrad[2, 2]
    stiff = 1.0 + stiffening_power * volume**2 - 2.0 / 3.0
    press = volume + stiffening_power * volume**3 / 3.0 - 2.0 / 3.0 * volume
    eye = jnp.eye(3, dtype=jnp.float32)
    stress = hgrad + jnp.transpose(hgrad, (1, 0, 2)) + press[None, None, :] * eye[:, :, None]
    force_vector = (
        jnp.einsum("ak,kce->ace", grads, stress, precision=lax.Precision.HIGHEST).reshape(
            24, element_count
        )
        + 0.25 * displacement
    )
    sym = grad_basis + jnp.transpose(grad_basis, (0, 2, 1, 3))
    trace_basis = grad_basis[:, 0, 0] + grad_basis[:, 1, 1] + grad_basis[:, 2, 2]
    mode_image = jnp.einsum("ak,ekcm->eacm", grads, sym, precision=lax.Precision.HIGHEST)
    mode_image = (
        mode_image
        + stiff[:, None, None, None] * grads[None, :, :, None] * trace_basis[:, None, None, :]
        + 0.25 * corner_nodes.astype(jnp.float32)
    )
    return (mode_image.reshape(element_count, 24, basis_modes), force_vector)


def local(basis, send_rows, elem_slot, set_size, elem_weight, element_stiffening, state, load):
    nodes = basis.shape[0]
    basis_modes = basis.shape[2]
    flat = basis.reshape(nodes, 3 * basis_modes)
    outgoing = jnp.take(flat, send_rows[0, 0], axis=0)
    arrived = lax.all_to_all(outgoing, "elem", split_axis=0, concat_axis=0, tiled=True)
    element_count = elem_slot.shape[1]
    chosen_elements = jnp.take(arrived, elem_slot.T.reshape(-1), axis=0)
    basis_matrix = chosen_elements.reshape(element_count, 24, basis_modes)
    set_index = lax.axis_index("elem")
    block_index = lax.axis_index("blk")
    live = lax.dynamic_index_in_dim(set_size, set_index, keepdims=False)
    position = block_index * element_count + jnp.arange(element_count, dtype=jnp.int32)
    weights = jnp.where(position < live, elem_weight, jnp.zeros_like(elem_weight))
    displacement = jnp.einsum("agd,d->ga", basis_matrix, state, preferred_element_type=jnp.float32)
    mode_image, force_vector = element_contributions(basis_matrix, displacement, element_stiffening)
    weighted_image = (weights[:, None, None] * mode_image).astype(jnp.bfloat16)
    weighted_force = (force_vector * weights[None, :]).astype(jnp.bfloat16)
    tangent = lax.dot_general(
        basis_matrix,
        weighted_image,
        (((0, 1), (0, 1)), ((), ())),
        preferred_element_type=jnp.float32,
    )
    force_all = lax.dot_general(
        basis_matrix,
        weighted_force,
        (((0, 1), (1, 0)), ((), ())),
        preferred_element_type=jnp.float32,
    )
    halfway, force_part = (
        lax.psum_scatter(tangent, "blk", scatter_dimension=1, tiled=True),
        lax.psum_scatter(force_all, "blk", scatter_dimension=0, tiled=True),
    )
    mine = lax.psum_scatter(halfway, "elem", scatter_dimension=0, tiled=True)
    force_cols = lax.psum(force_part, "elem")
    scale = lax.rsqrt(24.0 * jnp.sum(set_size).astype(jnp.float32))
    return (mine * scale, force_cols * scale - load)


def signs(corner):
    return [1.0 if corner >> axis & 1 else -1.0 for axis in range(3)]


def signed_sum(terms, sign):
    total = terms[0] if sign[0] > 0 else -terms[0]
    for term, one in zip(terms[1:], sign[1:]):
        total = total + term if one > 0 else total - term
    return total


def fused_kernel(
    devs,
    basis_hbm,
    send_hbm,
    slot_hbm,
    size_hbm,
    weight_hbm,
    stiff_hbm,
    state_hbm,
    load_hbm,
    tangent_ref,
    residual_ref,
    basis_ref,
    send_ref,
    slot_ref,
    size_ref,
    weight_ref,
    stiff_ref,
    state_ref,
    load_ref,
    in_sem,
    out_rows,
    arr,
    v_ref,
    vt_ref,
    w_ref,
    g_ref,
    force_ref,
    part,
    recv_core,
    mid,
    recv_first,
    recv_second,
    acc,
    recv_z,
    gather_send,
    gather_recv,
    core_send,
    core_recv,
    first_send,
    first_recv,
    second_send,
    second_recv,
    z_send,
    z_recv,
):
    nodes = basis_ref.shape[1]
    modes = basis_ref.shape[2]
    slots = arr.shape[1]
    cap = slots // devs
    elements = weight_ref.shape[1]
    corners = 8 * elements
    planes = devs // 2
    rows = modes // devs
    me = lax.axis_index("elem")
    blk = lax.axis_index("blk")
    x, z = lax.rem(me, 2), me // 2
    core, y = lax.rem(blk, 2), blk // 2
    core_peer = (me, y * 2 + 1 - core)
    y_peer = (me, (1 - y) * 2 + core)
    x_peer = (z * 2 + 1 - x, blk)

    def flipped(mask):
        dest, bit = 0, 1
        while bit < devs:
            low = lax.rem(me // bit, 2)
            dest = dest + bit * (1 - low if mask & bit else low)
            bit *= 2
        return dest

    loads = []
    for i, (src, dst) in enumerate(
        (
            (send_hbm, send_ref),
            (basis_hbm.at[0], basis_ref.at[0]),
            (basis_hbm.at[1], basis_ref.at[1]),
            (basis_hbm.at[2], basis_ref.at[2]),
            (slot_hbm, slot_ref),
            (size_hbm, size_ref),
            (weight_hbm, weight_ref),
            (stiff_hbm, stiff_ref),
            (state_hbm, state_ref),
            (load_hbm, load_ref),
        )
    ):
        copy = pltpu.make_async_copy(src, dst, in_sem.at[i])
        copy.start()
        loads.append(copy)

    barrier = pltpu.get_barrier_semaphore()
    for step in range(1, devs):
        pl.semaphore_signal(
            barrier, inc=1, device_id=(lax.rem(me + step, devs), blk), device_id_type=MESH
        )
    for peer in (core_peer, y_peer):
        pl.semaphore_signal(barrier, inc=1, device_id=peer, device_id_type=MESH)

    loads[0].wait()
    asked = jnp.broadcast_to(send_ref[...], (nodes, slots))
    pick_t = jnp.where(lax.broadcasted_iota(jnp.int32, (nodes, slots), 0) == asked, 1.0, 0.0)
    pick = jnp.transpose(pick_t).astype(jnp.bfloat16)
    mine = pl.ds(pl.multiple_of(me * cap, cap), cap)
    order = list(range(devs - 1, 0, -1))
    copies = [[], [], []]
    for c in range(3):
        loads[1 + c].wait()
        out_rows[c] = jnp.dot(
            pick, basis_ref[c], preferred_element_type=jnp.float32
        ).astype(jnp.bfloat16)
        if c == 0:
            pl.semaphore_wait(barrier, devs + 1)
        for mask in order:
            dest = flipped(mask)
            copy = pltpu.make_async_remote_copy(
                src_ref=out_rows.at[c, pl.ds(pl.multiple_of(dest * cap, cap), cap), :],
                dst_ref=arr.at[c, mine, :],
                send_sem=gather_send.at[c, mask - 1],
                recv_sem=gather_recv.at[c, mask - 1],
                device_id=(dest, blk),
                device_id_type=MESH,
            )
            copy.start()
            copies[c].append(copy)
        arr[c, mine, :] = out_rows[c, mine, :]

    for copy in loads[4:]:
        copy.wait()
    slot_row = jnp.concatenate([slot_ref[a : a + 1, :] for a in range(8)], axis=1)
    wanted = jnp.broadcast_to(slot_row, (slots, corners))
    spread_t = jnp.where(lax.broadcasted_iota(jnp.int32, (slots, corners), 0) == wanted, 1.0, 0.0)
    spread = jnp.transpose(spread_t)
    spread_t = spread_t.astype(jnp.bfloat16)
    by_corner = [spread[a * elements : (a + 1) * elements] for a in range(8)]
    coef = jnp.concatenate(
        [0.25 * signed_sum(by_corner, [signs(a)[k] for a in range(8)]) for k in range(3)], axis=0
    ).astype(jnp.bfloat16)
    spread = spread.astype(jnp.bfloat16)
    both = jnp.concatenate([weight_ref[...], stiff_ref[...]], axis=1)
    columns = jnp.transpose(jnp.broadcast_to(both, (LANES, 2 * elements)))
    live = size_ref[me]
    position = blk * elements + lax.broadcasted_iota(jnp.int32, (elements, LANES), 0)
    omega = jnp.where(position < live, columns[:elements], 0.0)
    stiffening = columns[elements:]
    state_rows = jnp.broadcast_to(state_ref[...].astype(jnp.float32), (LANES, modes)).astype(
        jnp.bfloat16
    )
    disp = []
    for c in range(3):
        for copy in copies[c]:
            copy.wait_recv()
        rows_c = arr[c]
        v = jnp.dot(spread, rows_c, preferred_element_type=jnp.float32).astype(jnp.bfloat16)
        v_ref[c] = v
        vt_ref[c] = lax.dot_general(
            rows_c, spread_t, (((0,), (0,)), ((), ())), preferred_element_type=jnp.float32
        ).astype(jnp.bfloat16)
        g_ref[c] = jnp.dot(coef, rows_c, preferred_element_type=jnp.float32)
        moved = lax.dot_general(
            v, state_rows, (((1,), (1,)), ((), ())), preferred_element_type=jnp.float32
        )
        disp.append([moved[a * elements : (a + 1) * elements] for a in range(8)])

    hgrad = [
        [0.25 * signed_sum(disp[c], [signs(a)[k] for a in range(8)]) for c in range(3)]
        for k in range(3)
    ]
    volume = hgrad[0][0] + hgrad[1][1] + hgrad[2][2]
    square = stiffening * volume * volume
    lam = 1.0 + square - 2.0 / 3.0
    press = volume + square * volume / 3.0 - 2.0 / 3.0 * volume
    quarter = 0.25 * omega

    force = jnp.zeros((LANES, modes), jnp.float32)
    for c in range(3):
        stress = [
            hgrad[k][c] + hgrad[c][k] + press if k == c else hgrad[k][c] + hgrad[c][k]
            for k in range(3)
        ]
        wforce = jnp.concatenate(
            [quarter * (signed_sum(stress, signs(a)) + disp[c][a]) for a in range(8)], axis=0
        ).astype(jnp.bfloat16)
        force = force + lax.dot_general(
            wforce, v_ref[c], (((0,), (0,)), ((), ())), preferred_element_type=jnp.float32
        )

    force_ref[...] = force[:8]
    for q in range(modes // LANES):
        lanes = pl.ds(q * LANES, LANES)
        grad = [
            [g_ref[c, pl.ds(k * elements, elements), lanes] for c in range(3)] for k in range(3)
        ]
        trace = lam * (grad[0][0] + grad[1][1] + grad[2][2])
        for c in range(3):
            terms = [
                quarter * (grad[k][c] + grad[c][k] + trace if k == c else grad[k][c] + grad[c][k])
                for k in range(3)
            ]
            for a in range(4):
                half = signed_sum(terms, signs(a))
                for corner, image in ((a, half), (7 - a, -half)):
                    at = pl.ds(corner * elements, elements)
                    w_ref[c, at, lanes] = (
                        image + quarter * v_ref[c, at, lanes].astype(jnp.float32)
                    ).astype(jnp.bfloat16)

    def fill(to_y, to_core):
        lanes = pl.ds(pl.multiple_of((to_y * 2 + to_core) * LANES, LANES), LANES)
        block = jnp.dot(vt_ref[0], w_ref[0, :, lanes], preferred_element_type=jnp.float32)
        for c in (1, 2):
            block = block + jnp.dot(
                vt_ref[c], w_ref[c, :, lanes], preferred_element_type=jnp.float32
            )
        tail = force_ref[:, lanes]
        for dest in range(devs):
            to_x, to_z = dest % 2, dest // 2
            p, zz = to_z // (planes // 2), to_z % (planes // 2)
            f, s = (to_y, to_x) if p == 0 else (to_x, to_y)
            part[p, to_core, f, s, zz, :rows] = block[dest * rows : (dest + 1) * rows]
            part[p, to_core, f, s, zz, rows:] = tail

    for to_y in range(2):
        fill(to_y, 1 - core)
    cores = []
    for p in range(2):
        copy = pltpu.make_async_remote_copy(
            src_ref=part.at[p, 1 - core],
            dst_ref=recv_core.at[p],
            send_sem=core_send.at[p],
            recv_sem=core_recv.at[p],
            device_id=core_peer,
            device_id_type=MESH,
        )
        copy.start()
        cores.append(copy)
    for to_y in range(2):
        fill(to_y, core)
    order = (((y, y_peer), (x, x_peer)), ((x, x_peer), (y, y_peer)))
    firsts = []
    for p in range(2):
        at, peer = order[p][0]
        cores[p].wait_recv()
        mid[p, 1 - at] = part[p, core, 1 - at] + recv_core[p, 1 - at]
        copy = pltpu.make_async_remote_copy(
            src_ref=mid.at[p, 1 - at],
            dst_ref=recv_first.at[p],
            send_sem=first_send.at[p],
            recv_sem=first_recv.at[p],
            device_id=peer,
            device_id_type=MESH,
        )
        copy.start()
        firsts.append(copy)
    seconds = []
    for p in range(2):
        at = order[p][0][0]
        there, peer = order[p][1]
        mid[p, at] = part[p, core, at] + recv_core[p, at]
        firsts[p].wait_recv()
        mid[p, at, 1 - there] = mid[p, at, 1 - there] + recv_first[p, 1 - there]
        copy = pltpu.make_async_remote_copy(
            src_ref=mid.at[p, at, 1 - there],
            dst_ref=recv_second.at[p],
            send_sem=second_send.at[p],
            recv_sem=second_recv.at[p],
            device_id=peer,
            device_id_type=MESH,
        )
        copy.start()
        seconds.append(copy)
    for p in range(2):
        at = order[p][0][0]
        there = order[p][1][0]
        seconds[p].wait_recv()
        acc[pl.ds(p * (planes // 2), planes // 2)] = (
            mid[p, at, there] + recv_first[p, there] + recv_second[p]
        )
    lasts = []
    for step in range(1, planes):
        dest = lax.rem(z + step, planes)
        copy = pltpu.make_async_remote_copy(
            src_ref=acc.at[dest],
            dst_ref=recv_z.at[step - 1],
            send_sem=z_send.at[step - 1],
            recv_sem=z_recv.at[step - 1],
            device_id=(dest * 2 + x, blk),
            device_id_type=MESH,
        )
        copy.start()
        lasts.append(copy)
    count = size_ref[0]
    for i in range(1, devs):
        count = count + size_ref[i]
    scale = lax.rsqrt(jnp.full((8, LANES), 24.0 * count.astype(jnp.float32), jnp.float32))
    total = acc[z]
    for step in range(1, planes):
        lasts[step - 1].wait_recv()
        total = total + recv_z[step - 1]
    tangent_ref[...] = total[:rows] * jnp.tile(scale, (rows // 8, 1))
    residual_ref[...] = (total[rows:] * scale)[:1] - load_ref[...]
    for copy in sum(copies, []) + cores + firsts + seconds + lasts:
        copy.wait_send()


def fused(devs, basis, send_rows, elem_slot, set_size, elem_weight, element_stiffening, state, load):
    nodes, _, modes = basis.shape
    slots = send_rows.shape[2]
    elements = elem_slot.shape[1]
    corners = 8 * elements
    rows = modes // devs
    half = devs // 4
    block = (half, rows + 8, LANES)
    f32, b16 = jnp.float32, jnp.bfloat16
    dma = pltpu.SemaphoreType.DMA
    vmem = pl.BlockSpec(memory_space=pltpu.VMEM)
    anywhere = pl.BlockSpec(memory_space=pl.ANY)
    tangent, residual = pl.pallas_call(
        functools.partial(fused_kernel, devs),
        out_shape=(
            jax.ShapeDtypeStruct((rows, LANES), f32),
            jax.ShapeDtypeStruct((1, LANES), f32),
        ),
        in_specs=[anywhere] * 8,
        out_specs=(vmem, vmem),
        scratch_shapes=[
            pltpu.VMEM((3, nodes, modes), b16),
            pltpu.VMEM((1, slots), jnp.int32),
            pltpu.VMEM((8, elements), jnp.int32),
            pltpu.SMEM(set_size.shape, jnp.int32),
            pltpu.VMEM((1, elements), f32),
            pltpu.VMEM((1, elements), f32),
            pltpu.VMEM((1, modes), b16),
            pltpu.VMEM((1, LANES), f32),
            dma((10,)),
            pltpu.VMEM((3, slots, modes), b16),
            pltpu.VMEM((3, slots, modes), b16),
            pltpu.VMEM((3, corners, modes), b16),
            pltpu.VMEM((3, modes, corners), b16),
            pltpu.VMEM((3, corners, modes), b16),
            pltpu.VMEM((3, 3 * elements, modes), f32),
            pltpu.VMEM((8, modes), f32),
            pltpu.VMEM((2, 2, 2, 2) + block, f32),
            pltpu.VMEM((2, 2, 2) + block, f32),
            pltpu.VMEM((2, 2, 2) + block, f32),
            pltpu.VMEM((2, 2) + block, f32),
            pltpu.VMEM((2,) + block, f32),
            pltpu.VMEM((devs // 2, rows + 8, LANES), f32),
            pltpu.VMEM((devs // 2 - 1, rows + 8, LANES), f32),
            dma((3, devs - 1)),
            dma((3, devs - 1)),
            dma((2,)),
            dma((2,)),
            dma((2,)),
            dma((2,)),
            dma((2,)),
            dma((2,)),
            dma((devs // 2 - 1,)),
            dma((devs // 2 - 1,)),
        ],
        compiler_params=pltpu.CompilerParams(
            collective_id=0, has_side_effects=True, vmem_limit_bytes=60 * 1024 * 1024
        ),
        cost_estimate=pl.CostEstimate(
            flops=6 * modes * modes * corners, bytes_accessed=2 * basis.size, transcendentals=0
        ),
        name="galerkin",
    )(
        jnp.transpose(basis, (1, 0, 2)),
        send_rows.reshape(1, slots),
        elem_slot,
        set_size,
        elem_weight.reshape(1, elements),
        element_stiffening.reshape(1, elements),
        state.reshape(1, modes),
        load.reshape(1, LANES),
    )
    return tangent, residual.reshape(LANES)


def solution(mesh):
    in_specs = (
        P("elem", None, None),
        P("elem", "blk", None),
        P(None, ("elem", "blk")),
        P(),
        P(("elem", "blk")),
        P(("elem", "blk")),
        P(),
        P("blk"),
    )
    out_specs = (P("elem", "blk"), P("blk"))
    devs, blocks = mesh.shape["elem"], mesh.shape["blk"]

    def run(*args):
        modes, slots, elements = args[0].shape[2], args[1].shape[2], args[2].shape[1] // mesh.size
        fits = (
            blocks == 4
            and modes == blocks * LANES
            and devs % 4 == 0
            and modes % (8 * devs) == 0
            and slots % (16 * devs) == 0
            and 2 * elements == LANES
        )
        part = functools.partial(fused, devs) if fits else local
        return jax.shard_map(
            part, mesh=mesh, in_specs=in_specs, out_specs=out_specs, check_vma=False
        )(*args)

    return run
```

```python
import functools

import jax
import jax.numpy as jnp
from jax import lax
from jax.experimental import pallas as pl
from jax.experimental.pallas import tpu as pltpu
from jax.sharding import PartitionSpec as P

LANES = 128
MESH = pl.DeviceIdType.MESH


def corner_grads():
    corner = jnp.arange(8)[:, None]
    bit = corner // 2 ** jnp.arange(3)[None, :] % 2
    return (bit * 2 - 1).astype(jnp.float32) * 0.25


def element_contributions(basis_matrix, displacement, stiffening_power):
    grads = corner_grads()
    element_count = basis_matrix.shape[0]
    basis_modes = basis_matrix.shape[2]
    corner_nodes = basis_matrix.reshape(element_count, 8, 3, basis_modes)
    grad_basis = jnp.einsum(
        "ak,eacm->ekcm",
        grads.astype(jnp.bfloat16),
        corner_nodes,
        preferred_element_type=jnp.float32,
    )
    moved = displacement.reshape(8, 3, element_count)
    hgrad = jnp.einsum("ak,ace->kce", grads, moved, precision=lax.Precision.HIGHEST)
    volume = hgrad[0, 0] + hgrad[1, 1] + hgrad[2, 2]
    stiff = 1.0 + stiffening_power * volume**2 - 2.0 / 3.0
    press = volume + stiffening_power * volume**3 / 3.0 - 2.0 / 3.0 * volume
    eye = jnp.eye(3, dtype=jnp.float32)
    stress = hgrad + jnp.transpose(hgrad, (1, 0, 2)) + press[None, None, :] * eye[:, :, None]
    force_vector = (
        jnp.einsum("ak,kce->ace", grads, stress, precision=lax.Precision.HIGHEST).reshape(
            24, element_count
        )
        + 0.25 * displacement
    )
    sym = grad_basis + jnp.transpose(grad_basis, (0, 2, 1, 3))
    trace_basis = grad_basis[:, 0, 0] + grad_basis[:, 1, 1] + grad_basis[:, 2, 2]
    mode_image = jnp.einsum("ak,ekcm->eacm", grads, sym, precision=lax.Precision.HIGHEST)
    mode_image = (
        mode_image
        + stiff[:, None, None, None] * grads[None, :, :, None] * trace_basis[:, None, None, :]
        + 0.25 * corner_nodes.astype(jnp.float32)
    )
    return (mode_image.reshape(element_count, 24, basis_modes), force_vector)


def local(basis, send_rows, elem_slot, set_size, elem_weight, element_stiffening, state, load):
    nodes = basis.shape[0]
    basis_modes = basis.shape[2]
    flat = basis.reshape(nodes, 3 * basis_modes)
    outgoing = jnp.take(flat, send_rows[0, 0], axis=0)
    arrived = lax.all_to_all(outgoing, "elem", split_axis=0, concat_axis=0, tiled=True)
    element_count = elem_slot.shape[1]
    chosen_elements = jnp.take(arrived, elem_slot.T.reshape(-1), axis=0)
    basis_matrix = chosen_elements.reshape(element_count, 24, basis_modes)
    set_index = lax.axis_index("elem")
    block_index = lax.axis_index("blk")
    live = lax.dynamic_index_in_dim(set_size, set_index, keepdims=False)
    position = block_index * element_count + jnp.arange(element_count, dtype=jnp.int32)
    weights = jnp.where(position < live, elem_weight, jnp.zeros_like(elem_weight))
    displacement = jnp.einsum("agd,d->ga", basis_matrix, state, preferred_element_type=jnp.float32)
    mode_image, force_vector = element_contributions(basis_matrix, displacement, element_stiffening)
    weighted_image = (weights[:, None, None] * mode_image).astype(jnp.bfloat16)
    weighted_force = (force_vector * weights[None, :]).astype(jnp.bfloat16)
    tangent = lax.dot_general(
        basis_matrix,
        weighted_image,
        (((0, 1), (0, 1)), ((), ())),
        preferred_element_type=jnp.float32,
    )
    force_all = lax.dot_general(
        basis_matrix,
        weighted_force,
        (((0, 1), (1, 0)), ((), ())),
        preferred_element_type=jnp.float32,
    )
    halfway, force_part = (
        lax.psum_scatter(tangent, "blk", scatter_dimension=1, tiled=True),
        lax.psum_scatter(force_all, "blk", scatter_dimension=0, tiled=True),
    )
    mine = lax.psum_scatter(halfway, "elem", scatter_dimension=0, tiled=True)
    force_cols = lax.psum(force_part, "elem")
    scale = lax.rsqrt(24.0 * jnp.sum(set_size).astype(jnp.float32))
    return (mine * scale, force_cols * scale - load)


def signs(corner):
    return [1.0 if corner >> axis & 1 else -1.0 for axis in range(3)]


def signed_sum(terms, sign):
    total = terms[0] if sign[0] > 0 else -terms[0]
    for term, one in zip(terms[1:], sign[1:]):
        total = total + term if one > 0 else total - term
    return total


def fused_kernel(
    devs,
    basis_hbm,
    send_hbm,
    slot_hbm,
    size_hbm,
    weight_hbm,
    stiff_hbm,
    state_hbm,
    load_hbm,
    tangent_ref,
    residual_ref,
    basis_ref,
    send_ref,
    slot_ref,
    size_ref,
    weight_ref,
    stiff_ref,
    state_ref,
    load_ref,
    out_rows,
    arr,
    disp_out,
    disp_in,
    vt_ref,
    w_ref,
    part,
    recv_core,
    mid,
    recv_first,
    recv_second,
    acc,
    recv_z,
    in_sem,
    gather_send,
    gather_recv,
    disp_send,
    disp_recv,
    core_send,
    core_recv,
    first_send,
    first_recv,
    second_send,
    second_recv,
    z_send,
    z_recv,
):
    nodes = basis_ref.shape[1]
    modes = basis_ref.shape[2]
    slots = arr.shape[1]
    cap = slots // devs
    elements = weight_ref.shape[1]
    corners = 8 * elements
    planes = devs // 2
    rows = modes // devs
    chunks = modes // LANES
    f32, b16 = jnp.float32, jnp.bfloat16
    me = lax.axis_index("elem")
    blk = lax.axis_index("blk")
    x, z = lax.rem(me, 2), me // 2
    core, y = lax.rem(blk, 2), blk // 2
    core_peer = (me, y * 2 + 1 - core)
    y_peer = (me, (1 - y) * 2 + core)
    x_peer = (z * 2 + 1 - x, blk)

    def flipped(mask):
        dest, bit = 0, 1
        while bit < devs:
            low = lax.rem(me // bit, 2)
            dest = dest + bit * (1 - low if mask & bit else low)
            bit *= 2
        return dest

    def remote(src, dst, send, recv, peer):
        copy = pltpu.make_async_remote_copy(
            src_ref=src,
            dst_ref=dst,
            send_sem=send,
            recv_sem=recv,
            device_id=peer,
            device_id_type=MESH,
        )
        copy.start()
        return copy

    loads = []
    for i, (src, dst) in enumerate(
        (
            (send_hbm, send_ref),
            (basis_hbm, basis_ref),
            (state_hbm, state_ref),
            (slot_hbm, slot_ref),
            (size_hbm, size_ref),
            (weight_hbm, weight_ref),
            (stiff_hbm, stiff_ref),
            (load_hbm, load_ref),
        )
    ):
        copy = pltpu.make_async_copy(src, dst, in_sem.at[i])
        copy.start()
        loads.append(copy)

    barrier = pltpu.get_barrier_semaphore()
    for step in range(1, devs):
        pl.semaphore_signal(
            barrier, inc=1, device_id=(lax.rem(me + step, devs), blk), device_id_type=MESH
        )
    for peer in (core_peer, y_peer):
        pl.semaphore_signal(barrier, inc=1, device_id=peer, device_id_type=MESH)

    loads[0].wait()
    asked = jnp.broadcast_to(send_ref[...], (nodes, slots))
    pick_t = jnp.where(lax.broadcasted_iota(jnp.int32, (nodes, slots), 0) == asked, 1.0, 0.0)
    pick = jnp.transpose(pick_t).astype(b16)
    mine = pl.ds(pl.multiple_of(me * cap, cap), cap)
    masks = list(range(devs - 1, 0, -1))
    gathers = [[] for _ in range(chunks)]

    def choose(q):
        lanes = pl.ds(q * LANES, LANES)
        for c in range(3):
            out_rows[q, :, c * LANES : (c + 1) * LANES] = jnp.dot(
                pick, basis_ref[c, :, lanes], preferred_element_type=f32
            ).astype(b16)

    def send(q):
        for mask in masks:
            dest = flipped(mask)
            theirs = pl.ds(pl.multiple_of(dest * cap, cap), cap)
            gathers[q].append(
                remote(
                    out_rows.at[q, theirs, :],
                    arr.at[q, mine, :],
                    gather_send.at[q, mask - 1],
                    gather_recv.at[q, mask - 1],
                    (dest, blk),
                )
            )
        arr[q, mine, :] = out_rows[q, mine, :]

    loads[1].wait()
    choose(0)
    pl.semaphore_wait(barrier, devs + 1)
    send(0)
    for q in range(1, chunks):
        choose(q)

    loads[2].wait()
    state = jnp.broadcast_to(state_ref[...].astype(f32).reshape(1, modes), (8, modes))
    component = lax.broadcasted_iota(jnp.int32, (8, modes), 0)
    moved = jnp.zeros((8, slots), f32)
    for c in range(3):
        state_c = jnp.where(component == c, state, 0.0).astype(b16)
        for q in range(chunks):
            moved = moved + lax.dot_general(
                state_c[:, q * LANES : (q + 1) * LANES],
                out_rows[q, :, c * LANES : (c + 1) * LANES],
                (((1,), (1,)), ((), ())),
                preferred_element_type=f32,
            )
    for tile in range(slots // LANES):
        disp_out[tile] = moved[:, tile * LANES : (tile + 1) * LANES]
    disps = []
    for mask in masks:
        dest = flipped(mask)
        disps.append(
            remote(
                disp_out.at[dest * cap // LANES],
                disp_in.at[me],
                disp_send.at[mask - 1],
                disp_recv.at[mask - 1],
                (dest, blk),
            )
        )
    disp_in[me] = disp_out[me * cap // LANES]
    for q in range(1, chunks):
        send(q)

    for copy in loads[3:]:
        copy.wait()
    slot_row = jnp.concatenate([slot_ref[a : a + 1, :] for a in range(8)], axis=1)
    wanted = jnp.broadcast_to(slot_row, (slots, corners))
    spread_t = jnp.where(lax.broadcasted_iota(jnp.int32, (slots, corners), 0) == wanted, 1.0, 0.0)
    spread = jnp.transpose(spread_t)
    spread_t = spread_t.astype(b16)
    by_corner = [spread[a * elements : (a + 1) * elements] for a in range(8)]
    coef = jnp.concatenate(
        [0.25 * signed_sum(by_corner, [signs(a)[k] for a in range(8)]) for k in range(3)], axis=0
    ).astype(b16)
    spread = spread.astype(b16)
    lane_row = slot_row + lax.div(slot_row, cap) * (LANES - cap) + lax.rem(me * cap, LANES)
    wide = (devs * LANES, corners)
    spread_disp = jnp.where(
        lax.broadcasted_iota(jnp.int32, wide, 0) == jnp.broadcast_to(lane_row, wide), 1.0, 0.0
    ).astype(b16)

    for copy in disps:
        copy.wait_recv()
    whole = jnp.concatenate([disp_in[j] for j in range(devs)], axis=1)
    high = whole.astype(b16).astype(f32)
    middle = (whole - high).astype(b16).astype(f32)
    low = whole - high - middle
    pieces = jnp.dot(
        jnp.concatenate([high, middle, low], axis=0).astype(b16),
        spread_disp,
        preferred_element_type=f32,
    )
    picked = pieces[:8] + pieces[8:16] + pieces[16:24]
    disp = [
        [picked[c : c + 1, a * elements : (a + 1) * elements] for a in range(8)] for c in range(3)
    ]
    hgrad = [
        [0.25 * signed_sum(disp[c], [signs(a)[k] for a in range(8)]) for c in range(3)]
        for k in range(3)
    ]
    position = blk * elements + lax.broadcasted_iota(jnp.int32, (1, elements), 1)
    omega = jnp.where(position < size_ref[me], weight_ref[...], 0.0)
    volume = hgrad[0][0] + hgrad[1][1] + hgrad[2][2]
    square = stiff_ref[...] * volume * volume
    lam = 1.0 + square - 2.0 / 3.0
    press = volume + square * volume / 3.0 - 2.0 / 3.0 * volume
    wforce = []
    for c in range(3):
        stress = [
            hgrad[k][c] + hgrad[c][k] + press if k == c else hgrad[k][c] + hgrad[c][k]
            for k in range(3)
        ]
        row = jnp.concatenate(
            [0.25 * omega * (signed_sum(stress, signs(a)) + disp[c][a]) for a in range(8)], axis=1
        )
        wforce.append(jnp.broadcast_to(row, (8, corners)).astype(b16))
    both = jnp.concatenate([0.25 * omega, lam], axis=1)
    columns = jnp.transpose(jnp.broadcast_to(both, (LANES, 2 * elements)))
    quarter, lam = columns[:elements], columns[elements:]

    def place(i, j, block, tail):
        to_y, to_core = j // 2, j % 2
        for to_x in range(2):
            f, s = (to_y, to_x) if i % 2 == 0 else (to_x, to_y)
            part[i, to_core, f, s, :rows] = block[to_x * rows : (to_x + 1) * rows]
            part[i, to_core, f, s, rows:] = tail

    def half_of(ref, i, to_y):
        return ref.at[to_y] if i % 2 == 0 else ref.at[:, to_y]

    tails = []
    cores = [[] for _ in range(planes)]
    for q in range(chunks):
        lanes = pl.ds(q * LANES, LANES)
        for copy in gathers[q]:
            copy.wait_recv()
        arrived = arr[q]
        vt = lax.dot_general(
            arrived, spread_t, (((0,), (0,)), ((), ())), preferred_element_type=f32
        ).astype(b16)
        v = jnp.dot(spread, arrived, preferred_element_type=f32)
        g = jnp.dot(coef, arrived, preferred_element_type=f32)
        grad = [
            [
                g[k * elements : (k + 1) * elements, c * LANES : (c + 1) * LANES]
                for c in range(3)
            ]
            for k in range(3)
        ]
        trace = lam * (grad[0][0] + grad[1][1] + grad[2][2])
        tail = jnp.zeros((8, LANES), f32)
        for c in range(3):
            vt_ref[c, lanes, :] = vt[c * LANES : (c + 1) * LANES]
            v_c = v[:, c * LANES : (c + 1) * LANES]
            terms = [
                grad[k][c] + grad[c][k] + trace if k == c else grad[k][c] + grad[c][k]
                for k in range(3)
            ]
            for a in range(4):
                half = signed_sum(terms, signs(a))
                for corner, image in ((a, half), (7 - a, -half)):
                    at = corner * elements
                    w_ref[c, pl.ds(at, elements), lanes] = (
                        quarter * (image + v_c[at : at + elements])
                    ).astype(b16)
            tail = tail + jnp.dot(wforce[c], v_c.astype(b16), preferred_element_type=f32)
        tails.append(tail)
        down = sum(
            jnp.dot(
                vt_ref[c, : (q + 1) * LANES, :], w_ref[c, :, lanes], preferred_element_type=f32
            )
            for c in range(3)
        )
        for i in range(q + 1):
            place(i, q, down[i * LANES : (i + 1) * LANES], tail)
        if q > 0:
            across = sum(
                jnp.dot(
                    vt_ref[c, lanes, :], w_ref[c, :, : q * LANES], preferred_element_type=f32
                )
                for c in range(3)
            )
            for j in range(q):
                place(q, j, across[:, j * LANES : (j + 1) * LANES], tails[j])
        for i in range(planes):
            for to_y in range(2):
                if max(i, 2 * to_y + 1) == q:
                    cores[i].append(
                        remote(
                            half_of(part.at[i, 1 - core], i, to_y),
                            half_of(recv_core.at[i], i, to_y),
                            core_send.at[i, to_y],
                            core_recv.at[i, to_y],
                            core_peer,
                        )
                    )

    firsts, seconds = [], []
    order = (((y, y_peer), (x, x_peer)), ((x, x_peer), (y, y_peer)))
    for i in range(planes):
        at, peer = order[i % 2][0]
        for copy in cores[i]:
            copy.wait_recv()
        mid[i, 1 - at] = part[i, core, 1 - at] + recv_core[i, 1 - at]
        firsts.append(
            remote(mid.at[i, 1 - at], recv_first.at[i], first_send.at[i], first_recv.at[i], peer)
        )
    for i in range(planes):
        at = order[i % 2][0][0]
        there, peer = order[i % 2][1]
        mid[i, at] = part[i, core, at] + recv_core[i, at]
        firsts[i].wait_recv()
        mid[i, at, 1 - there] = mid[i, at, 1 - there] + recv_first[i, 1 - there]
        seconds.append(
            remote(
                mid.at[i, at, 1 - there],
                recv_second.at[i],
                second_send.at[i],
                second_recv.at[i],
                peer,
            )
        )

    def z_copy(i):
        slot = lax.rem(z - i + planes - 1, planes)
        return pltpu.make_async_remote_copy(
            src_ref=acc.at[i],
            dst_ref=recv_z.at[slot],
            send_sem=z_send.at[i],
            recv_sem=z_recv.at[slot],
            device_id=(i * 2 + x, blk),
            device_id_type=MESH,
        )

    for i in range(planes):
        at = order[i % 2][0][0]
        there = order[i % 2][1][0]
        seconds[i].wait_recv()
        acc[i] = mid[i, at, there] + recv_first[i, there] + recv_second[i]

        @pl.when(z != i)
        def _(i=i):
            z_copy(i).start()

    count = size_ref[0]
    for i in range(1, devs):
        count = count + size_ref[i]
    scale = lax.rsqrt(jnp.full((8, LANES), 24.0 * count.astype(f32), f32))
    total = acc[z]
    for slot in range(planes - 1):
        pltpu.make_async_remote_copy(
            src_ref=acc.at[slot],
            dst_ref=recv_z.at[slot],
            send_sem=z_send.at[slot],
            recv_sem=z_recv.at[slot],
            device_id=x_peer,
            device_id_type=MESH,
        ).wait_recv()
        total = total + recv_z[slot]
    tangent_ref[...] = total[:rows] * jnp.tile(scale, (rows // 8, 1))
    residual_ref[...] = (total[rows:] * scale)[:1] - load_ref[...]
    for copy in sum(gathers, []) + disps + sum(cores, []) + firsts + seconds:
        copy.wait_send()
    for i in range(planes):

        @pl.when(z != i)
        def _(i=i):
            z_copy(i).wait_send()


def fused(devs, basis, send_rows, elem_slot, set_size, elem_weight, element_stiffening, state, load):
    nodes, _, modes = basis.shape
    slots = send_rows.shape[2]
    elements = elem_slot.shape[1]
    corners = 8 * elements
    rows = modes // devs
    planes = devs // 2
    chunks = modes // LANES
    block = (rows + 8, LANES)
    f32, b16 = jnp.float32, jnp.bfloat16
    dma = pltpu.SemaphoreType.DMA
    vmem = pl.BlockSpec(memory_space=pltpu.VMEM)
    anywhere = pl.BlockSpec(memory_space=pl.ANY)
    tangent, residual = pl.pallas_call(
        functools.partial(fused_kernel, devs),
        out_shape=(
            jax.ShapeDtypeStruct((rows, LANES), f32),
            jax.ShapeDtypeStruct((1, LANES), f32),
        ),
        in_specs=[anywhere] * 8,
        out_specs=(vmem, vmem),
        scratch_shapes=[
            pltpu.VMEM((3, nodes, modes), b16),
            pltpu.VMEM((1, slots), jnp.int32),
            pltpu.VMEM((8, elements), jnp.int32),
            pltpu.SMEM(set_size.shape, jnp.int32),
            pltpu.VMEM((1, elements), f32),
            pltpu.VMEM((1, elements), f32),
            pltpu.VMEM((modes,), b16),
            pltpu.VMEM((1, LANES), f32),
            pltpu.VMEM((chunks, slots, 3 * LANES), b16),
            pltpu.VMEM((chunks, slots, 3 * LANES), b16),
            pltpu.VMEM((slots // LANES, 8, LANES), f32),
            pltpu.VMEM((devs, 8, LANES), f32),
            pltpu.VMEM((3, modes, corners), b16),
            pltpu.VMEM((3, corners, modes), b16),
            pltpu.VMEM((planes, 2, 2, 2) + block, f32),
            pltpu.VMEM((planes, 2, 2) + block, f32),
            pltpu.VMEM((planes, 2, 2) + block, f32),
            pltpu.VMEM((planes, 2) + block, f32),
            pltpu.VMEM((planes,) + block, f32),
            pltpu.VMEM((planes,) + block, f32),
            pltpu.VMEM((planes - 1,) + block, f32),
            dma((8,)),
            dma((chunks, devs - 1)),
            dma((chunks, devs - 1)),
            dma((devs - 1,)),
            dma((devs - 1,)),
            dma((planes, 2)),
            dma((planes, 2)),
            dma((planes,)),
            dma((planes,)),
            dma((planes,)),
            dma((planes,)),
            dma((planes,)),
            dma((planes - 1,)),
        ],
        compiler_params=pltpu.CompilerParams(
            collective_id=0, has_side_effects=True, vmem_limit_bytes=60 * 1024 * 1024
        ),
        cost_estimate=pl.CostEstimate(
            flops=6 * modes * modes * corners, bytes_accessed=2 * basis.size, transcendentals=0
        ),
        name="galerkin",
    )(
        jnp.transpose(basis, (1, 0, 2)),
        send_rows.reshape(1, slots),
        elem_slot,
        set_size,
        elem_weight.reshape(1, elements),
        element_stiffening.reshape(1, elements),
        state,
        load.reshape(1, LANES),
    )
    return tangent, residual.reshape(LANES)


def solution(mesh):
    in_specs = (
        P("elem", None, None),
        P("elem", "blk", None),
        P(None, ("elem", "blk")),
        P(),
        P(("elem", "blk")),
        P(("elem", "blk")),
        P(),
        P("blk"),
    )
    out_specs = (P("elem", "blk"), P("blk"))
    devs, blocks = mesh.shape["elem"], mesh.shape["blk"]

    def run(*args):
        modes, slots, elements = args[0].shape[2], args[1].shape[2], args[2].shape[1] // mesh.size
        fits = (
            blocks == 4
            and modes == blocks * LANES
            and devs == 2 * blocks
            and modes % (8 * devs) == 0
            and slots % (16 * devs) == 0
            and 2 * elements == LANES
            and slots % LANES == 0
            and LANES % (slots // devs) == 0
        )
        part = functools.partial(fused, devs) if fits else local
        return jax.shard_map(
            part, mesh=mesh, in_specs=in_specs, out_specs=out_specs, check_vma=False
        )(*args)

    return run
```

```python
import functools

import jax
import jax.numpy as jnp
from jax import lax
from jax.experimental import pallas as pl
from jax.experimental.pallas import tpu as pltpu
from jax.sharding import PartitionSpec as P

LANES = 128
MESH = pl.DeviceIdType.MESH


def corner_grads():
    corner = jnp.arange(8)[:, None]
    bit = corner // 2 ** jnp.arange(3)[None, :] % 2
    return (bit * 2 - 1).astype(jnp.float32) * 0.25


def element_contributions(basis_matrix, displacement, stiffening_power):
    grads = corner_grads()
    element_count = basis_matrix.shape[0]
    basis_modes = basis_matrix.shape[2]
    corner_nodes = basis_matrix.reshape(element_count, 8, 3, basis_modes)
    grad_basis = jnp.einsum(
        "ak,eacm->ekcm",
        grads.astype(jnp.bfloat16),
        corner_nodes,
        preferred_element_type=jnp.float32,
    )
    moved = displacement.reshape(8, 3, element_count)
    hgrad = jnp.einsum("ak,ace->kce", grads, moved, precision=lax.Precision.HIGHEST)
    volume = hgrad[0, 0] + hgrad[1, 1] + hgrad[2, 2]
    stiff = 1.0 + stiffening_power * volume**2 - 2.0 / 3.0
    press = volume + stiffening_power * volume**3 / 3.0 - 2.0 / 3.0 * volume
    eye = jnp.eye(3, dtype=jnp.float32)
    stress = hgrad + jnp.transpose(hgrad, (1, 0, 2)) + press[None, None, :] * eye[:, :, None]
    force_vector = (
        jnp.einsum("ak,kce->ace", grads, stress, precision=lax.Precision.HIGHEST).reshape(
            24, element_count
        )
        + 0.25 * displacement
    )
    sym = grad_basis + jnp.transpose(grad_basis, (0, 2, 1, 3))
    trace_basis = grad_basis[:, 0, 0] + grad_basis[:, 1, 1] + grad_basis[:, 2, 2]
    mode_image = jnp.einsum("ak,ekcm->eacm", grads, sym, precision=lax.Precision.HIGHEST)
    mode_image = (
        mode_image
        + stiff[:, None, None, None] * grads[None, :, :, None] * trace_basis[:, None, None, :]
        + 0.25 * corner_nodes.astype(jnp.float32)
    )
    return (mode_image.reshape(element_count, 24, basis_modes), force_vector)


def local(basis, send_rows, elem_slot, set_size, elem_weight, element_stiffening, state, load):
    nodes = basis.shape[0]
    basis_modes = basis.shape[2]
    flat = basis.reshape(nodes, 3 * basis_modes)
    outgoing = jnp.take(flat, send_rows[0, 0], axis=0)
    arrived = lax.all_to_all(outgoing, "elem", split_axis=0, concat_axis=0, tiled=True)
    element_count = elem_slot.shape[1]
    chosen_elements = jnp.take(arrived, elem_slot.T.reshape(-1), axis=0)
    basis_matrix = chosen_elements.reshape(element_count, 24, basis_modes)
    set_index = lax.axis_index("elem")
    block_index = lax.axis_index("blk")
    live = lax.dynamic_index_in_dim(set_size, set_index, keepdims=False)
    position = block_index * element_count + jnp.arange(element_count, dtype=jnp.int32)
    weights = jnp.where(position < live, elem_weight, jnp.zeros_like(elem_weight))
    displacement = jnp.einsum("agd,d->ga", basis_matrix, state, preferred_element_type=jnp.float32)
    mode_image, force_vector = element_contributions(basis_matrix, displacement, element_stiffening)
    weighted_image = (weights[:, None, None] * mode_image).astype(jnp.bfloat16)
    weighted_force = (force_vector * weights[None, :]).astype(jnp.bfloat16)
    tangent = lax.dot_general(
        basis_matrix,
        weighted_image,
        (((0, 1), (0, 1)), ((), ())),
        preferred_element_type=jnp.float32,
    )
    force_all = lax.dot_general(
        basis_matrix,
        weighted_force,
        (((0, 1), (1, 0)), ((), ())),
        preferred_element_type=jnp.float32,
    )
    halfway, force_part = (
        lax.psum_scatter(tangent, "blk", scatter_dimension=1, tiled=True),
        lax.psum_scatter(force_all, "blk", scatter_dimension=0, tiled=True),
    )
    mine = lax.psum_scatter(halfway, "elem", scatter_dimension=0, tiled=True)
    force_cols = lax.psum(force_part, "elem")
    scale = lax.rsqrt(24.0 * jnp.sum(set_size).astype(jnp.float32))
    return (mine * scale, force_cols * scale - load)


def signs(corner):
    return [1.0 if corner >> axis & 1 else -1.0 for axis in range(3)]


def signed_sum(terms, sign):
    total = terms[0] if sign[0] > 0 else -terms[0]
    for term, one in zip(terms[1:], sign[1:]):
        total = total + term if one > 0 else total - term
    return total


def fused_kernel(
    devs,
    basis_hbm,
    send_hbm,
    slot_hbm,
    size_hbm,
    weight_hbm,
    stiff_hbm,
    state_hbm,
    load_hbm,
    tangent_ref,
    residual_ref,
    basis_ref,
    send_ref,
    slot_ref,
    size_ref,
    weight_ref,
    stiff_ref,
    state_ref,
    load_ref,
    out_rows,
    arr,
    disp_out,
    disp_in,
    vt_ref,
    w_ref,
    part,
    recv_core,
    mid,
    recv_first,
    recv_second,
    acc,
    recv_z,
    in_sem,
    gather_send,
    gather_recv,
    disp_send,
    disp_recv,
    core_send,
    core_recv,
    first_send,
    first_recv,
    second_send,
    second_recv,
    z_send,
    z_recv,
):
    nodes = basis_ref.shape[1]
    modes = basis_ref.shape[2]
    slots = arr.shape[1]
    cap = slots // devs
    elements = weight_ref.shape[1]
    corners = 8 * elements
    planes = devs // 2
    rows = modes // devs
    chunks = modes // LANES
    f32, b16 = jnp.float32, jnp.bfloat16
    me = lax.axis_index("elem")
    blk = lax.axis_index("blk")
    x, z = lax.rem(me, 2), me // 2
    core, y = lax.rem(blk, 2), blk // 2
    core_peer = (me, y * 2 + 1 - core)
    y_peer = (me, (1 - y) * 2 + core)
    x_peer = (z * 2 + 1 - x, blk)

    def flipped(mask):
        dest, bit = 0, 1
        while bit < devs:
            low = lax.rem(me // bit, 2)
            dest = dest + bit * (1 - low if mask & bit else low)
            bit *= 2
        return dest

    def remote(src, dst, send, recv, peer):
        copy = pltpu.make_async_remote_copy(
            src_ref=src,
            dst_ref=dst,
            send_sem=send,
            recv_sem=recv,
            device_id=peer,
            device_id_type=MESH,
        )
        copy.start()
        return copy

    def by_lanes(q):
        return pl.ds(q * LANES, LANES)

    loads = []
    for i, (src, dst) in enumerate(
        (
            (send_hbm, send_ref),
            *(
                (basis_hbm.at[:, :, by_lanes(q)], basis_ref.at[:, :, by_lanes(q)])
                for q in range(chunks)
            ),
            (state_hbm, state_ref),
            (slot_hbm, slot_ref),
            (size_hbm, size_ref),
            (weight_hbm, weight_ref),
            (stiff_hbm, stiff_ref),
            (load_hbm, load_ref),
        )
    ):
        copy = pltpu.make_async_copy(src, dst, in_sem.at[i])
        copy.start()
        loads.append(copy)

    barrier = pltpu.get_barrier_semaphore()
    for step in range(1, devs):
        pl.semaphore_signal(
            barrier, inc=1, device_id=(lax.rem(me + step, devs), blk), device_id_type=MESH
        )
    for peer in (core_peer, y_peer):
        pl.semaphore_signal(barrier, inc=1, device_id=peer, device_id_type=MESH)

    loads[0].wait()
    asked = jnp.broadcast_to(send_ref[...], (nodes, slots))
    pick_t = jnp.where(lax.broadcasted_iota(jnp.int32, (nodes, slots), 0) == asked, 1.0, 0.0)
    pick = jnp.transpose(pick_t).astype(b16)
    mine = pl.ds(pl.multiple_of(me * cap, cap), cap)
    masks = list(range(devs - 1, 0, -1))
    gathers = [[] for _ in range(chunks)]

    def choose(q):
        loads[1 + q].wait()
        lanes = by_lanes(q)
        for c in range(3):
            out_rows[q, :, c * LANES : (c + 1) * LANES] = jnp.dot(
                pick, basis_ref[c, :, lanes], preferred_element_type=f32
            ).astype(b16)

    def send(q):
        for mask in masks:
            dest = flipped(mask)
            theirs = pl.ds(pl.multiple_of(dest * cap, cap), cap)
            gathers[q].append(
                remote(
                    out_rows.at[q, theirs, :],
                    arr.at[q, mine, :],
                    gather_send.at[q, mask - 1],
                    gather_recv.at[q, mask - 1],
                    (dest, blk),
                )
            )
        arr[q, mine, :] = out_rows[q, mine, :]

    choose(0)
    pl.semaphore_wait(barrier, devs + 1)
    send(0)
    for q in range(1, chunks):
        choose(q)

    loads[1 + chunks].wait()
    state = jnp.broadcast_to(state_ref[...].astype(f32).reshape(1, modes), (8, modes))
    component = lax.broadcasted_iota(jnp.int32, (8, modes), 0)
    moved = jnp.zeros((8, slots), f32)
    for c in range(3):
        state_c = jnp.where(component == c, state, 0.0).astype(b16)
        for q in range(chunks):
            moved = moved + lax.dot_general(
                state_c[:, q * LANES : (q + 1) * LANES],
                out_rows[q, :, c * LANES : (c + 1) * LANES],
                (((1,), (1,)), ((), ())),
                preferred_element_type=f32,
            )
    for tile in range(slots // LANES):
        disp_out[tile] = moved[:, tile * LANES : (tile + 1) * LANES]
    disps = []
    for mask in masks:
        dest = flipped(mask)
        disps.append(
            remote(
                disp_out.at[dest * cap // LANES],
                disp_in.at[me],
                disp_send.at[mask - 1],
                disp_recv.at[mask - 1],
                (dest, blk),
            )
        )
    disp_in[me] = disp_out[me * cap // LANES]
    for q in range(1, chunks):
        send(q)

    for copy in loads[2 + chunks :]:
        copy.wait()
    slot_row = jnp.concatenate([slot_ref[a : a + 1, :] for a in range(8)], axis=1)
    wanted = jnp.broadcast_to(slot_row, (slots, corners))
    spread_t = jnp.where(lax.broadcasted_iota(jnp.int32, (slots, corners), 0) == wanted, 1.0, 0.0)
    spread = jnp.transpose(spread_t)
    spread_t = spread_t.astype(b16)
    by_corner = [spread[a * elements : (a + 1) * elements] for a in range(8)]
    coef = jnp.concatenate(
        [0.25 * signed_sum(by_corner, [signs(a)[k] for a in range(8)]) for k in range(3)], axis=0
    ).astype(b16)
    spread = spread.astype(b16)
    lane_row = slot_row + lax.div(slot_row, cap) * (LANES - cap) + lax.rem(me * cap, LANES)
    wide = (devs * LANES, corners)
    spread_disp = jnp.where(
        lax.broadcasted_iota(jnp.int32, wide, 0) == jnp.broadcast_to(lane_row, wide), 1.0, 0.0
    ).astype(b16)

    for copy in disps:
        copy.wait_recv()
    whole = jnp.concatenate([disp_in[j] for j in range(devs)], axis=1)
    high = whole.astype(b16).astype(f32)
    middle = (whole - high).astype(b16).astype(f32)
    low = whole - high - middle
    pieces = jnp.dot(
        jnp.concatenate([high, middle, low], axis=0).astype(b16),
        spread_disp,
        preferred_element_type=f32,
    )
    picked = pieces[:8] + pieces[8:16] + pieces[16:24]
    disp = [
        [picked[c : c + 1, a * elements : (a + 1) * elements] for a in range(8)] for c in range(3)
    ]
    hgrad = [
        [0.25 * signed_sum(disp[c], [signs(a)[k] for a in range(8)]) for c in range(3)]
        for k in range(3)
    ]
    position = blk * elements + lax.broadcasted_iota(jnp.int32, (1, elements), 1)
    omega = jnp.where(position < size_ref[me], weight_ref[...], 0.0)
    volume = hgrad[0][0] + hgrad[1][1] + hgrad[2][2]
    square = stiff_ref[...] * volume * volume
    lam = 1.0 + square - 2.0 / 3.0
    press = volume + square * volume / 3.0 - 2.0 / 3.0 * volume
    wforce = []
    for c in range(3):
        stress = [
            hgrad[k][c] + hgrad[c][k] + press if k == c else hgrad[k][c] + hgrad[c][k]
            for k in range(3)
        ]
        row = jnp.concatenate(
            [0.25 * omega * (signed_sum(stress, signs(a)) + disp[c][a]) for a in range(8)], axis=1
        )
        wforce.append(jnp.broadcast_to(row, (8, corners)).astype(b16))
    both = jnp.concatenate([0.25 * omega, lam], axis=1)
    columns = jnp.transpose(jnp.broadcast_to(both, (LANES, 2 * elements)))
    quarter, lam = columns[:elements], columns[elements:]

    def place(i, j, block, tail):
        to_y, to_core = j // 2, j % 2
        for to_x in range(2):
            f, s = (to_y, to_x) if i == planes - 1 else (to_x, to_y)
            part[i, to_core, f, s, :rows] = block[to_x * rows : (to_x + 1) * rows]
            part[i, to_core, f, s, rows:] = tail

    def half_of(ref, i, to_y):
        return ref.at[to_y] if i == planes - 1 else ref.at[:, to_y]

    def to_other_core(q, which):
        for i in which:
            for to_y in range(2):
                if max(i, 2 * to_y + 1) == q:
                    cores[i].append(
                        remote(
                            half_of(part.at[i, 1 - core], i, to_y),
                            half_of(recv_core.at[i], i, to_y),
                            core_send.at[i, to_y],
                            core_recv.at[i, to_y],
                            core_peer,
                        )
                    )

    def first(i, to_y):
        mid[i, 1 - x, to_y] = part[i, core, 1 - x, to_y] + recv_core[i, 1 - x, to_y]
        firsts[i].append(
            remote(
                mid.at[i, 1 - x, to_y],
                recv_first.at[i, to_y],
                first_send.at[i, to_y],
                first_recv.at[i, to_y],
                x_peer,
            )
        )

    tails = []
    cores = [[] for _ in range(planes)]
    firsts = [[] for _ in range(planes)]
    for q in range(chunks):
        lanes = pl.ds(q * LANES, LANES)
        if q == chunks - 1:
            for i in range(planes - 1):
                cores[i][0].wait_recv()
                first(i, 0)
        for copy in gathers[q]:
            copy.wait_recv()
        arrived = arr[q]
        vt = lax.dot_general(
            arrived, spread_t, (((0,), (0,)), ((), ())), preferred_element_type=f32
        ).astype(b16)
        v = jnp.dot(spread, arrived, preferred_element_type=f32)
        g = jnp.dot(coef, arrived, preferred_element_type=f32)
        grad = [
            [
                g[k * elements : (k + 1) * elements, c * LANES : (c + 1) * LANES]
                for c in range(3)
            ]
            for k in range(3)
        ]
        trace = lam * (grad[0][0] + grad[1][1] + grad[2][2])
        tail = jnp.zeros((8, LANES), f32)
        for c in range(3):
            vt_ref[c, lanes, :] = vt[c * LANES : (c + 1) * LANES]
            v_c = v[:, c * LANES : (c + 1) * LANES]
            terms = [
                grad[k][c] + grad[c][k] + trace if k == c else grad[k][c] + grad[c][k]
                for k in range(3)
            ]
            for a in range(4):
                half = signed_sum(terms, signs(a))
                for corner, image in ((a, half), (7 - a, -half)):
                    at = corner * elements
                    w_ref[c, pl.ds(at, elements), lanes] = (
                        quarter * (image + v_c[at : at + elements])
                    ).astype(b16)
            tail = tail + jnp.dot(wforce[c], v_c.astype(b16), preferred_element_type=f32)
        tails.append(tail)
        down = sum(
            jnp.dot(
                vt_ref[c, : (q + 1) * LANES, :], w_ref[c, :, lanes], preferred_element_type=f32
            )
            for c in range(3)
        )
        for i in range(q + 1):
            place(i, q, down[i * LANES : (i + 1) * LANES], tail)
        to_other_core(q, range(q))
        if q > 0:
            across = sum(
                jnp.dot(
                    vt_ref[c, lanes, :], w_ref[c, :, : q * LANES], preferred_element_type=f32
                )
                for c in range(3)
            )
            for j in range(q):
                place(q, j, across[:, j * LANES : (j + 1) * LANES], tails[j])
            to_other_core(q, (q,))

    for i in range(planes - 1):
        cores[i][1].wait_recv()
        first(i, 1)
    at, peer = y, y_peer
    last = planes - 1
    for copy in cores[last]:
        copy.wait_recv()
    mid[last, 1 - at] = part[last, core, 1 - at] + recv_core[last, 1 - at]
    firsts[last].append(
        remote(
            mid.at[last, 1 - at],
            recv_first.at[last],
            first_send.at[last, 0],
            first_recv.at[last, 0],
            peer,
        )
    )
    seconds = []
    order = [((x, x_peer), (y, y_peer))] * (planes - 1) + [((y, y_peer), (x, x_peer))]
    for i in range(planes):
        at = order[i][0][0]
        there, peer = order[i][1]
        mid[i, at] = part[i, core, at] + recv_core[i, at]
        for copy in firsts[i]:
            copy.wait_recv()
        mid[i, at, 1 - there] = mid[i, at, 1 - there] + recv_first[i, 1 - there]
        seconds.append(
            remote(
                mid.at[i, at, 1 - there],
                recv_second.at[i],
                second_send.at[i],
                second_recv.at[i],
                peer,
            )
        )

    def z_copy(i):
        slot = lax.rem(z - i + planes - 1, planes)
        return pltpu.make_async_remote_copy(
            src_ref=acc.at[i],
            dst_ref=recv_z.at[slot],
            send_sem=z_send.at[i],
            recv_sem=z_recv.at[slot],
            device_id=(i * 2 + x, blk),
            device_id_type=MESH,
        )

    for i in range(planes):
        at = order[i][0][0]
        there = order[i][1][0]
        seconds[i].wait_recv()
        acc[i] = mid[i, at, there] + recv_first[i, there] + recv_second[i]

        @pl.when(z != i)
        def _(i=i):
            z_copy(i).start()

    count = size_ref[0]
    for i in range(1, devs):
        count = count + size_ref[i]
    scale = lax.rsqrt(jnp.full((8, LANES), 24.0 * count.astype(f32), f32))
    total = acc[z]
    for slot in range(planes - 1):
        pltpu.make_async_remote_copy(
            src_ref=acc.at[slot],
            dst_ref=recv_z.at[slot],
            send_sem=z_send.at[slot],
            recv_sem=z_recv.at[slot],
            device_id=x_peer,
            device_id_type=MESH,
        ).wait_recv()
        total = total + recv_z[slot]
    tangent_ref[...] = total[:rows] * jnp.tile(scale, (rows // 8, 1))
    residual_ref[...] = (total[rows:] * scale)[:1] - load_ref[...]
    for copy in sum(gathers, []) + disps + sum(cores, []) + sum(firsts, []) + seconds:
        copy.wait_send()
    for i in range(planes):

        @pl.when(z != i)
        def _(i=i):
            z_copy(i).wait_send()


def hand_on(tangent_ref, residual_ref, tangent_out, residual_out, sem):
    copies = [
        pltpu.make_async_copy(tangent_ref, tangent_out, sem.at[0]),
        pltpu.make_async_copy(residual_ref, residual_out, sem.at[1]),
    ]
    for copy in copies:
        copy.start()
    for copy in copies:
        copy.wait()


def fused(devs, basis, send_rows, elem_slot, set_size, elem_weight, element_stiffening, state, load):
    nodes, _, modes = basis.shape
    slots = send_rows.shape[2]
    elements = elem_slot.shape[1]
    corners = 8 * elements
    rows = modes // devs
    planes = devs // 2
    chunks = modes // LANES
    block = (rows + 8, LANES)
    f32, b16 = jnp.float32, jnp.bfloat16
    dma = pltpu.SemaphoreType.DMA
    vmem = pl.BlockSpec(memory_space=pltpu.VMEM)
    anywhere = pl.BlockSpec(memory_space=pl.ANY)
    tangent, residual = pl.pallas_call(
        functools.partial(fused_kernel, devs),
        out_shape=(
            jax.ShapeDtypeStruct((rows, LANES), f32),
            jax.ShapeDtypeStruct((1, LANES), f32),
        ),
        in_specs=[anywhere] * 8,
        out_specs=(vmem, vmem),
        scratch_shapes=[
            pltpu.VMEM((3, nodes, modes), b16),
            pltpu.VMEM((1, slots), jnp.int32),
            pltpu.VMEM((8, elements), jnp.int32),
            pltpu.SMEM(set_size.shape, jnp.int32),
            pltpu.VMEM((1, elements), f32),
            pltpu.VMEM((1, elements), f32),
            pltpu.VMEM((modes,), b16),
            pltpu.VMEM((1, LANES), f32),
            pltpu.VMEM((chunks, slots, 3 * LANES), b16),
            pltpu.VMEM((chunks, slots, 3 * LANES), b16),
            pltpu.VMEM((slots // LANES, 8, LANES), f32),
            pltpu.VMEM((devs, 8, LANES), f32),
            pltpu.VMEM((3, modes, corners), b16),
            pltpu.VMEM((3, corners, modes), b16),
            pltpu.VMEM((planes, 2, 2, 2) + block, f32),
            pltpu.VMEM((planes, 2, 2) + block, f32),
            pltpu.VMEM((planes, 2, 2) + block, f32),
            pltpu.VMEM((planes, 2) + block, f32),
            pltpu.VMEM((planes,) + block, f32),
            pltpu.VMEM((planes,) + block, f32),
            pltpu.VMEM((planes - 1,) + block, f32),
            dma((7 + chunks,)),
            dma((chunks, devs - 1)),
            dma((chunks, devs - 1)),
            dma((devs - 1,)),
            dma((devs - 1,)),
            dma((planes, 2)),
            dma((planes, 2)),
            dma((planes, 2)),
            dma((planes, 2)),
            dma((planes,)),
            dma((planes,)),
            dma((planes,)),
            dma((planes - 1,)),
        ],
        compiler_params=pltpu.CompilerParams(
            collective_id=0, has_side_effects=True, vmem_limit_bytes=60 * 1024 * 1024
        ),
        cost_estimate=pl.CostEstimate(
            flops=6 * modes * modes * corners, bytes_accessed=2 * basis.size, transcendentals=0
        ),
        name="galerkin",
    )(
        jnp.transpose(basis, (1, 0, 2)),
        send_rows.reshape(1, slots),
        elem_slot,
        set_size,
        elem_weight.reshape(1, elements),
        element_stiffening.reshape(1, elements),
        state,
        load.reshape(1, LANES),
    )
    tangent, residual = pl.pallas_call(
        hand_on,
        out_shape=(
            jax.ShapeDtypeStruct(tangent.shape, f32),
            jax.ShapeDtypeStruct(residual.shape, f32),
        ),
        in_specs=[anywhere] * 2,
        out_specs=(anywhere, anywhere),
        scratch_shapes=[dma((2,))],
        compiler_params=pltpu.CompilerParams(vmem_limit_bytes=60 * 1024 * 1024),
        name="hand_on",
    )(tangent, residual)
    return tangent, residual.reshape(LANES)


def solution(mesh):
    in_specs = (
        P("elem", None, None),
        P("elem", "blk", None),
        P(None, ("elem", "blk")),
        P(),
        P(("elem", "blk")),
        P(("elem", "blk")),
        P(),
        P("blk"),
    )
    out_specs = (P("elem", "blk"), P("blk"))
    devs, blocks = mesh.shape["elem"], mesh.shape["blk"]

    def run(*args):
        modes, slots, elements = args[0].shape[2], args[1].shape[2], args[2].shape[1] // mesh.size
        fits = (
            blocks == 4
            and modes == blocks * LANES
            and devs == 2 * blocks
            and modes % (8 * devs) == 0
            and slots % (16 * devs) == 0
            and 2 * elements == LANES
            and slots % LANES == 0
            and LANES % (slots // devs) == 0
        )
        part = functools.partial(fused, devs) if fits else local
        return jax.shard_map(
            part, mesh=mesh, in_specs=in_specs, out_specs=out_specs, check_vma=False
        )(*args)

    return run
```

```python
import functools

import jax
import jax.numpy as jnp
from jax import lax
from jax.experimental import pallas as pl
from jax.experimental.pallas import tpu as pltpu
from jax.sharding import PartitionSpec as P

LANES = 128
MESH = pl.DeviceIdType.MESH


def corner_grads():
    corner = jnp.arange(8)[:, None]
    bit = corner // 2 ** jnp.arange(3)[None, :] % 2
    return (bit * 2 - 1).astype(jnp.float32) * 0.25


def element_contributions(basis_matrix, displacement, stiffening_power):
    grads = corner_grads()
    element_count = basis_matrix.shape[0]
    basis_modes = basis_matrix.shape[2]
    corner_nodes = basis_matrix.reshape(element_count, 8, 3, basis_modes)
    grad_basis = jnp.einsum(
        "ak,eacm->ekcm",
        grads.astype(jnp.bfloat16),
        corner_nodes,
        preferred_element_type=jnp.float32,
    )
    moved = displacement.reshape(8, 3, element_count)
    hgrad = jnp.einsum("ak,ace->kce", grads, moved, precision=lax.Precision.HIGHEST)
    volume = hgrad[0, 0] + hgrad[1, 1] + hgrad[2, 2]
    stiff = 1.0 + stiffening_power * volume**2 - 2.0 / 3.0
    press = volume + stiffening_power * volume**3 / 3.0 - 2.0 / 3.0 * volume
    eye = jnp.eye(3, dtype=jnp.float32)
    stress = hgrad + jnp.transpose(hgrad, (1, 0, 2)) + press[None, None, :] * eye[:, :, None]
    force_vector = (
        jnp.einsum("ak,kce->ace", grads, stress, precision=lax.Precision.HIGHEST).reshape(
            24, element_count
        )
        + 0.25 * displacement
    )
    sym = grad_basis + jnp.transpose(grad_basis, (0, 2, 1, 3))
    trace_basis = grad_basis[:, 0, 0] + grad_basis[:, 1, 1] + grad_basis[:, 2, 2]
    mode_image = jnp.einsum("ak,ekcm->eacm", grads, sym, precision=lax.Precision.HIGHEST)
    mode_image = (
        mode_image
        + stiff[:, None, None, None] * grads[None, :, :, None] * trace_basis[:, None, None, :]
        + 0.25 * corner_nodes.astype(jnp.float32)
    )
    return (mode_image.reshape(element_count, 24, basis_modes), force_vector)


def local(basis, send_rows, elem_slot, set_size, elem_weight, element_stiffening, state, load):
    nodes = basis.shape[0]
    basis_modes = basis.shape[2]
    flat = basis.reshape(nodes, 3 * basis_modes)
    outgoing = jnp.take(flat, send_rows[0, 0], axis=0)
    arrived = lax.all_to_all(outgoing, "elem", split_axis=0, concat_axis=0, tiled=True)
    element_count = elem_slot.shape[1]
    chosen_elements = jnp.take(arrived, elem_slot.T.reshape(-1), axis=0)
    basis_matrix = chosen_elements.reshape(element_count, 24, basis_modes)
    set_index = lax.axis_index("elem")
    block_index = lax.axis_index("blk")
    live = lax.dynamic_index_in_dim(set_size, set_index, keepdims=False)
    position = block_index * element_count + jnp.arange(element_count, dtype=jnp.int32)
    weights = jnp.where(position < live, elem_weight, jnp.zeros_like(elem_weight))
    displacement = jnp.einsum("agd,d->ga", basis_matrix, state, preferred_element_type=jnp.float32)
    mode_image, force_vector = element_contributions(basis_matrix, displacement, element_stiffening)
    weighted_image = (weights[:, None, None] * mode_image).astype(jnp.bfloat16)
    weighted_force = (force_vector * weights[None, :]).astype(jnp.bfloat16)
    tangent = lax.dot_general(
        basis_matrix,
        weighted_image,
        (((0, 1), (0, 1)), ((), ())),
        preferred_element_type=jnp.float32,
    )
    force_all = lax.dot_general(
        basis_matrix,
        weighted_force,
        (((0, 1), (1, 0)), ((), ())),
        preferred_element_type=jnp.float32,
    )
    halfway, force_part = (
        lax.psum_scatter(tangent, "blk", scatter_dimension=1, tiled=True),
        lax.psum_scatter(force_all, "blk", scatter_dimension=0, tiled=True),
    )
    mine = lax.psum_scatter(halfway, "elem", scatter_dimension=0, tiled=True)
    force_cols = lax.psum(force_part, "elem")
    scale = lax.rsqrt(24.0 * jnp.sum(set_size).astype(jnp.float32))
    return (mine * scale, force_cols * scale - load)


def signs(corner):
    return [1.0 if corner >> axis & 1 else -1.0 for axis in range(3)]


def signed_sum(terms, sign):
    total = terms[0] if sign[0] > 0 else -terms[0]
    for term, one in zip(terms[1:], sign[1:]):
        total = total + term if one > 0 else total - term
    return total


def fused_kernel(
    devs,
    basis_hbm,
    send_hbm,
    slot_hbm,
    size_hbm,
    weight_hbm,
    stiff_hbm,
    state_hbm,
    load_hbm,
    tangent_ref,
    residual_ref,
    basis_ref,
    send_ref,
    slot_ref,
    size_ref,
    weight_ref,
    stiff_ref,
    state_ref,
    load_ref,
    out_rows,
    arr,
    disp_out,
    disp_in,
    vt_ref,
    w_ref,
    part,
    recv_core,
    mid,
    recv_first,
    recv_second,
    acc,
    recv_z,
    in_sem,
    gather_send,
    gather_recv,
    disp_send,
    disp_recv,
    core_send,
    core_recv,
    first_send,
    first_recv,
    second_send,
    second_recv,
    z_send,
    z_recv,
):
    nodes = basis_ref.shape[1]
    modes = basis_ref.shape[2]
    slots = arr.shape[1]
    cap = slots // devs
    elements = weight_ref.shape[1]
    corners = 8 * elements
    planes = devs // 2
    rows = modes // devs
    chunks = modes // LANES
    f32, b16 = jnp.float32, jnp.bfloat16
    me = lax.axis_index("elem")
    blk = lax.axis_index("blk")
    x, z = lax.rem(me, 2), me // 2
    core, y = lax.rem(blk, 2), blk // 2
    core_peer = (me, y * 2 + 1 - core)
    y_peer = (me, (1 - y) * 2 + core)
    x_peer = (z * 2 + 1 - x, blk)

    def flipped(mask):
        dest, bit = 0, 1
        while bit < devs:
            low = lax.rem(me // bit, 2)
            dest = dest + bit * (1 - low if mask & bit else low)
            bit *= 2
        return dest

    def remote(src, dst, send, recv, peer):
        copy = pltpu.make_async_remote_copy(
            src_ref=src,
            dst_ref=dst,
            send_sem=send,
            recv_sem=recv,
            device_id=peer,
            device_id_type=MESH,
        )
        copy.start()
        return copy

    def by_lanes(q):
        return pl.ds(q * LANES, LANES)

    loads = []
    for i, (src, dst) in enumerate(
        (
            (send_hbm, send_ref),
            *(
                (basis_hbm.at[:, :, by_lanes(q)], basis_ref.at[:, :, by_lanes(q)])
                for q in range(chunks)
            ),
            (state_hbm, state_ref),
            (slot_hbm, slot_ref),
            (size_hbm, size_ref),
            (weight_hbm, weight_ref),
            (stiff_hbm, stiff_ref),
            (load_hbm, load_ref),
        )
    ):
        copy = pltpu.make_async_copy(src, dst, in_sem.at[i])
        copy.start()
        loads.append(copy)

    barrier = pltpu.get_barrier_semaphore()
    for step in range(1, devs):
        pl.semaphore_signal(
            barrier, inc=1, device_id=(lax.rem(me + step, devs), blk), device_id_type=MESH
        )
    for peer in (core_peer, y_peer):
        pl.semaphore_signal(barrier, inc=1, device_id=peer, device_id_type=MESH)

    loads[0].wait()
    asked = jnp.broadcast_to(send_ref[...], (nodes, slots))
    pick_t = jnp.where(lax.broadcasted_iota(jnp.int32, (nodes, slots), 0) == asked, 1.0, 0.0)
    pick = jnp.transpose(pick_t).astype(b16)
    mine = pl.ds(pl.multiple_of(me * cap, cap), cap)
    masks = list(range(devs - 1, 0, -1))
    gathers = [[] for _ in range(chunks)]

    def choose(q):
        loads[1 + q].wait()
        lanes = by_lanes(q)
        for c in range(3):
            out_rows[q, :, c * LANES : (c + 1) * LANES] = jnp.dot(
                pick, basis_ref[c, :, lanes], preferred_element_type=f32
            ).astype(b16)

    def send(q):
        for mask in masks:
            dest = flipped(mask)
            theirs = pl.ds(pl.multiple_of(dest * cap, cap), cap)
            gathers[q].append(
                remote(
                    out_rows.at[q, theirs, :],
                    arr.at[q, mine, :],
                    gather_send.at[q, mask - 1],
                    gather_recv.at[q, mask - 1],
                    (dest, blk),
                )
            )
        arr[q, mine, :] = out_rows[q, mine, :]

    choose(0)
    pl.semaphore_wait(barrier, devs + 1)
    send(0)
    for q in range(1, chunks):
        choose(q)

    loads[1 + chunks].wait()
    state = jnp.broadcast_to(state_ref[...].astype(f32).reshape(1, modes), (8, modes))
    component = lax.broadcasted_iota(jnp.int32, (8, modes), 0)
    moved = jnp.zeros((8, slots), f32)
    for c in range(3):
        state_c = jnp.where(component == c, state, 0.0).astype(b16)
        for q in range(chunks):
            moved = moved + lax.dot_general(
                state_c[:, q * LANES : (q + 1) * LANES],
                out_rows[q, :, c * LANES : (c + 1) * LANES],
                (((1,), (1,)), ((), ())),
                preferred_element_type=f32,
            )
    for tile in range(slots // LANES):
        disp_out[tile] = moved[:, tile * LANES : (tile + 1) * LANES]
    disps = []
    for mask in masks:
        dest = flipped(mask)
        disps.append(
            remote(
                disp_out.at[dest * cap // LANES],
                disp_in.at[me],
                disp_send.at[mask - 1],
                disp_recv.at[mask - 1],
                (dest, blk),
            )
        )
    disp_in[me] = disp_out[me * cap // LANES]
    for q in range(1, chunks):
        send(q)

    for copy in loads[2 + chunks :]:
        copy.wait()
    slot_row = jnp.concatenate([slot_ref[a : a + 1, :] for a in range(8)], axis=1)
    wanted = jnp.broadcast_to(slot_row, (slots, corners))
    spread_t = jnp.where(lax.broadcasted_iota(jnp.int32, (slots, corners), 0) == wanted, 1.0, 0.0)
    spread = jnp.transpose(spread_t)
    spread_t = spread_t.astype(b16)
    by_corner = [spread[a * elements : (a + 1) * elements] for a in range(8)]
    coef = jnp.concatenate(
        [0.25 * signed_sum(by_corner, [signs(a)[k] for a in range(8)]) for k in range(3)], axis=0
    ).astype(b16)
    spread = spread.astype(b16)
    lane_row = slot_row + lax.div(slot_row, cap) * (LANES - cap) + lax.rem(me * cap, LANES)
    wide = (devs * LANES, corners)
    spread_disp = jnp.where(
        lax.broadcasted_iota(jnp.int32, wide, 0) == jnp.broadcast_to(lane_row, wide), 1.0, 0.0
    ).astype(b16)

    for copy in disps:
        copy.wait_recv()
    whole = jnp.concatenate([disp_in[j] for j in range(devs)], axis=1)
    high = whole.astype(b16).astype(f32)
    middle = (whole - high).astype(b16).astype(f32)
    low = whole - high - middle
    pieces = jnp.dot(
        jnp.concatenate([high, middle, low], axis=0).astype(b16),
        spread_disp,
        preferred_element_type=f32,
    )
    picked = pieces[:8] + pieces[8:16] + pieces[16:24]
    disp = [
        [picked[c : c + 1, a * elements : (a + 1) * elements] for a in range(8)] for c in range(3)
    ]
    hgrad = [
        [0.25 * signed_sum(disp[c], [signs(a)[k] for a in range(8)]) for c in range(3)]
        for k in range(3)
    ]
    position = blk * elements + lax.broadcasted_iota(jnp.int32, (1, elements), 1)
    omega = jnp.where(position < size_ref[me], weight_ref[...], 0.0)
    volume = hgrad[0][0] + hgrad[1][1] + hgrad[2][2]
    square = stiff_ref[...] * volume * volume
    lam = 1.0 + square - 2.0 / 3.0
    press = volume + square * volume / 3.0 - 2.0 / 3.0 * volume
    wforce = []
    for c in range(3):
        stress = [
            hgrad[k][c] + hgrad[c][k] + press if k == c else hgrad[k][c] + hgrad[c][k]
            for k in range(3)
        ]
        row = jnp.concatenate(
            [0.25 * omega * (signed_sum(stress, signs(a)) + disp[c][a]) for a in range(8)], axis=1
        )
        wforce.append(jnp.broadcast_to(row, (8, corners)).astype(b16))
    both = jnp.concatenate([0.25 * omega, lam], axis=1)
    columns = jnp.transpose(jnp.broadcast_to(both, (LANES, 2 * elements)))
    quarter, lam = columns[:elements], columns[elements:]

    def place(i, j, block, tail):
        to_y, to_core = j // 2, j % 2
        for to_x in range(2):
            part[i, to_core, to_x, to_y, :rows] = block[to_x * rows : (to_x + 1) * rows]
            part[i, to_core, to_x, to_y, rows:] = tail

    def to_other_core(q, which):
        for i in which:
            for to_y in range(2):
                if max(i, 2 * to_y + 1) == q:
                    cores[i].append(
                        remote(
                            part.at[i, 1 - core, :, to_y],
                            recv_core.at[i, :, to_y],
                            core_send.at[i, to_y],
                            core_recv.at[i, to_y],
                            core_peer,
                        )
                    )

    def first(i, to_y):
        mid[i, 1 - x, to_y] = part[i, core, 1 - x, to_y] + recv_core[i, 1 - x, to_y]
        firsts[i].append(
            remote(
                mid.at[i, 1 - x, to_y],
                recv_first.at[i, to_y],
                first_send.at[i, to_y],
                first_recv.at[i, to_y],
                x_peer,
            )
        )

    tails = []
    cores = [[] for _ in range(planes)]
    firsts = [[] for _ in range(planes)]
    for q in range(chunks):
        lanes = pl.ds(q * LANES, LANES)
        if q == chunks - 1:
            for i in range(planes - 1):
                cores[i][0].wait_recv()
                first(i, 0)
        for copy in gathers[q]:
            copy.wait_recv()
        arrived = arr[q]
        vt = lax.dot_general(
            arrived, spread_t, (((0,), (0,)), ((), ())), preferred_element_type=f32
        ).astype(b16)
        v = jnp.dot(spread, arrived, preferred_element_type=f32)
        g = jnp.dot(coef, arrived, preferred_element_type=f32)
        grad = [
            [
                g[k * elements : (k + 1) * elements, c * LANES : (c + 1) * LANES]
                for c in range(3)
            ]
            for k in range(3)
        ]
        trace = lam * (grad[0][0] + grad[1][1] + grad[2][2])
        tail = jnp.zeros((8, LANES), f32)
        for c in range(3):
            vt_ref[c, lanes, :] = vt[c * LANES : (c + 1) * LANES]
            v_c = v[:, c * LANES : (c + 1) * LANES]
            terms = [
                grad[k][c] + grad[c][k] + trace if k == c else grad[k][c] + grad[c][k]
                for k in range(3)
            ]
            for a in range(4):
                half = signed_sum(terms, signs(a))
                for corner, image in ((a, half), (7 - a, -half)):
                    at = corner * elements
                    w_ref[c, pl.ds(at, elements), lanes] = (
                        quarter * (image + v_c[at : at + elements])
                    ).astype(b16)
            tail = tail + jnp.dot(wforce[c], v_c.astype(b16), preferred_element_type=f32)
        tails.append(tail)
        down = sum(
            jnp.dot(
                vt_ref[c, : (q + 1) * LANES, :], w_ref[c, :, lanes], preferred_element_type=f32
            )
            for c in range(3)
        )
        for i in range(q + 1):
            place(i, q, down[i * LANES : (i + 1) * LANES], tail)
        to_other_core(q, range(q))
        if q > 0:
            across = sum(
                jnp.dot(
                    vt_ref[c, lanes, :], w_ref[c, :, : q * LANES], preferred_element_type=f32
                )
                for c in range(3)
            )
            for j in range(q):
                place(q, j, across[:, j * LANES : (j + 1) * LANES], tails[j])
            to_other_core(q, (q,))

    for i in range(planes):
        for to_y in range(len(firsts[i]), 2):
            cores[i][to_y].wait_recv()
            first(i, to_y)
    seconds = []

    def second(i):
        mid[i, x] = part[i, core, x] + recv_core[i, x]
        for copy in firsts[i]:
            copy.wait_recv()
        mid[i, x, 1 - y] = mid[i, x, 1 - y] + recv_first[i, 1 - y]
        seconds.append(
            remote(
                mid.at[i, x, 1 - y],
                recv_second.at[i],
                second_send.at[i],
                second_recv.at[i],
                y_peer,
            )
        )

    def z_copy(i):
        slot = lax.rem(z - i + planes - 1, planes)
        return pltpu.make_async_remote_copy(
            src_ref=acc.at[i],
            dst_ref=recv_z.at[slot],
            send_sem=z_send.at[i],
            recv_sem=z_recv.at[slot],
            device_id=(i * 2 + x, blk),
            device_id_type=MESH,
        )

    def third(i):
        seconds[i].wait_recv()
        acc[i] = mid[i, x, y] + recv_first[i, y] + recv_second[i]

        @pl.when(z != i)
        def _():
            z_copy(i).start()

    second(0)
    for i in range(1, planes):
        second(i)
        third(i - 1)
    third(planes - 1)

    count = size_ref[0]
    for i in range(1, devs):
        count = count + size_ref[i]
    scale = lax.rsqrt(jnp.full((8, LANES), 24.0 * count.astype(f32), f32))
    total = acc[z]
    for slot in range(planes - 1):
        pltpu.make_async_remote_copy(
            src_ref=acc.at[slot],
            dst_ref=recv_z.at[slot],
            send_sem=z_send.at[slot],
            recv_sem=z_recv.at[slot],
            device_id=x_peer,
            device_id_type=MESH,
        ).wait_recv()
        total = total + recv_z[slot]
    tangent_ref[...] = total[:rows] * jnp.tile(scale, (rows // 8, 1))
    residual_ref[...] = (total[rows:] * scale)[:1] - load_ref[...]
    for copy in sum(gathers, []) + disps + sum(cores, []) + sum(firsts, []) + seconds:
        copy.wait_send()
    for i in range(planes):

        @pl.when(z != i)
        def _(i=i):
            z_copy(i).wait_send()


def hand_on(tangent_ref, residual_ref, tangent_out, residual_out, sem):
    copies = [
        pltpu.make_async_copy(tangent_ref, tangent_out, sem.at[0]),
        pltpu.make_async_copy(residual_ref, residual_out, sem.at[1]),
    ]
    for copy in copies:
        copy.start()
    for copy in copies:
        copy.wait()


def fused(devs, basis, send_rows, elem_slot, set_size, elem_weight, element_stiffening, state, load):
    nodes, _, modes = basis.shape
    slots = send_rows.shape[2]
    elements = elem_slot.shape[1]
    corners = 8 * elements
    rows = modes // devs
    planes = devs // 2
    chunks = modes // LANES
    block = (rows + 8, LANES)
    f32, b16 = jnp.float32, jnp.bfloat16
    dma = pltpu.SemaphoreType.DMA
    vmem = pl.BlockSpec(memory_space=pltpu.VMEM)
    anywhere = pl.BlockSpec(memory_space=pl.ANY)
    tangent, residual = pl.pallas_call(
        functools.partial(fused_kernel, devs),
        out_shape=(
            jax.ShapeDtypeStruct((rows, LANES), f32),
            jax.ShapeDtypeStruct((1, LANES), f32),
        ),
        in_specs=[anywhere] * 8,
        out_specs=(vmem, vmem),
        scratch_shapes=[
            pltpu.VMEM((3, nodes, modes), b16),
            pltpu.VMEM((1, slots), jnp.int32),
            pltpu.VMEM((8, elements), jnp.int32),
            pltpu.SMEM(set_size.shape, jnp.int32),
            pltpu.VMEM((1, elements), f32),
            pltpu.VMEM((1, elements), f32),
            pltpu.VMEM((modes,), b16),
            pltpu.VMEM((1, LANES), f32),
            pltpu.VMEM((chunks, slots, 3 * LANES), b16),
            pltpu.VMEM((chunks, slots, 3 * LANES), b16),
            pltpu.VMEM((slots // LANES, 8, LANES), f32),
            pltpu.VMEM((devs, 8, LANES), f32),
            pltpu.VMEM((3, modes, corners), b16),
            pltpu.VMEM((3, corners, modes), b16),
            pltpu.VMEM((planes, 2, 2, 2) + block, f32),
            pltpu.VMEM((planes, 2, 2) + block, f32),
            pltpu.VMEM((planes, 2, 2) + block, f32),
            pltpu.VMEM((planes, 2) + block, f32),
            pltpu.VMEM((planes,) + block, f32),
            pltpu.VMEM((planes,) + block, f32),
            pltpu.VMEM((planes - 1,) + block, f32),
            dma((7 + chunks,)),
            dma((chunks, devs - 1)),
            dma((chunks, devs - 1)),
            dma((devs - 1,)),
            dma((devs - 1,)),
            dma((planes, 2)),
            dma((planes, 2)),
            dma((planes, 2)),
            dma((planes, 2)),
            dma((planes,)),
            dma((planes,)),
            dma((planes,)),
            dma((planes - 1,)),
        ],
        compiler_params=pltpu.CompilerParams(
            collective_id=0, has_side_effects=True, vmem_limit_bytes=60 * 1024 * 1024
        ),
        cost_estimate=pl.CostEstimate(
            flops=6 * modes * modes * corners, bytes_accessed=2 * basis.size, transcendentals=0
        ),
        name="galerkin",
    )(
        jnp.transpose(basis, (1, 0, 2)),
        send_rows.reshape(1, slots),
        elem_slot,
        set_size,
        elem_weight.reshape(1, elements),
        element_stiffening.reshape(1, elements),
        state,
        load.reshape(1, LANES),
    )
    tangent, residual = pl.pallas_call(
        hand_on,
        out_shape=(
            jax.ShapeDtypeStruct(tangent.shape, f32),
            jax.ShapeDtypeStruct(residual.shape, f32),
        ),
        in_specs=[anywhere] * 2,
        out_specs=(anywhere, anywhere),
        scratch_shapes=[dma((2,))],
        compiler_params=pltpu.CompilerParams(vmem_limit_bytes=60 * 1024 * 1024),
        name="hand_on",
    )(tangent, residual)
    return tangent, residual.reshape(LANES)


def solution(mesh):
    in_specs = (
        P("elem", None, None),
        P("elem", "blk", None),
        P(None, ("elem", "blk")),
        P(),
        P(("elem", "blk")),
        P(("elem", "blk")),
        P(),
        P("blk"),
    )
    out_specs = (P("elem", "blk"), P("blk"))
    devs, blocks = mesh.shape["elem"], mesh.shape["blk"]

    def run(*args):
        modes, slots, elements = args[0].shape[2], args[1].shape[2], args[2].shape[1] // mesh.size
        fits = (
            blocks == 4
            and modes == blocks * LANES
            and devs == 2 * blocks
            and modes % (8 * devs) == 0
            and slots % (16 * devs) == 0
            and 2 * elements == LANES
            and slots % LANES == 0
            and LANES % (slots // devs) == 0
        )
        part = functools.partial(fused, devs) if fits else local
        return jax.shard_map(
            part, mesh=mesh, in_specs=in_specs, out_specs=out_specs, check_vma=False
        )(*args)

    return run
```

```python
import functools

import jax
import jax.numpy as jnp
from jax import lax
from jax.experimental import pallas as pl
from jax.experimental.pallas import tpu as pltpu
from jax.sharding import PartitionSpec as P

LANES = 128
MESH = pl.DeviceIdType.MESH


def corner_grads():
    corner = jnp.arange(8)[:, None]
    bit = corner // 2 ** jnp.arange(3)[None, :] % 2
    return (bit * 2 - 1).astype(jnp.float32) * 0.25


def element_contributions(basis_matrix, displacement, stiffening_power):
    grads = corner_grads()
    element_count = basis_matrix.shape[0]
    basis_modes = basis_matrix.shape[2]
    corner_nodes = basis_matrix.reshape(element_count, 8, 3, basis_modes)
    grad_basis = jnp.einsum(
        "ak,eacm->ekcm",
        grads.astype(jnp.bfloat16),
        corner_nodes,
        preferred_element_type=jnp.float32,
    )
    moved = displacement.reshape(8, 3, element_count)
    hgrad = jnp.einsum("ak,ace->kce", grads, moved, precision=lax.Precision.HIGHEST)
    volume = hgrad[0, 0] + hgrad[1, 1] + hgrad[2, 2]
    stiff = 1.0 + stiffening_power * volume**2 - 2.0 / 3.0
    press = volume + stiffening_power * volume**3 / 3.0 - 2.0 / 3.0 * volume
    eye = jnp.eye(3, dtype=jnp.float32)
    stress = hgrad + jnp.transpose(hgrad, (1, 0, 2)) + press[None, None, :] * eye[:, :, None]
    force_vector = (
        jnp.einsum("ak,kce->ace", grads, stress, precision=lax.Precision.HIGHEST).reshape(
            24, element_count
        )
        + 0.25 * displacement
    )
    sym = grad_basis + jnp.transpose(grad_basis, (0, 2, 1, 3))
    trace_basis = grad_basis[:, 0, 0] + grad_basis[:, 1, 1] + grad_basis[:, 2, 2]
    mode_image = jnp.einsum("ak,ekcm->eacm", grads, sym, precision=lax.Precision.HIGHEST)
    mode_image = (
        mode_image
        + stiff[:, None, None, None] * grads[None, :, :, None] * trace_basis[:, None, None, :]
        + 0.25 * corner_nodes.astype(jnp.float32)
    )
    return (mode_image.reshape(element_count, 24, basis_modes), force_vector)


def local(basis, send_rows, elem_slot, set_size, elem_weight, element_stiffening, state, load):
    nodes = basis.shape[0]
    basis_modes = basis.shape[2]
    flat = basis.reshape(nodes, 3 * basis_modes)
    outgoing = jnp.take(flat, send_rows[0, 0], axis=0)
    arrived = lax.all_to_all(outgoing, "elem", split_axis=0, concat_axis=0, tiled=True)
    element_count = elem_slot.shape[1]
    chosen_elements = jnp.take(arrived, elem_slot.T.reshape(-1), axis=0)
    basis_matrix = chosen_elements.reshape(element_count, 24, basis_modes)
    set_index = lax.axis_index("elem")
    block_index = lax.axis_index("blk")
    live = lax.dynamic_index_in_dim(set_size, set_index, keepdims=False)
    position = block_index * element_count + jnp.arange(element_count, dtype=jnp.int32)
    weights = jnp.where(position < live, elem_weight, jnp.zeros_like(elem_weight))
    displacement = jnp.einsum("agd,d->ga", basis_matrix, state, preferred_element_type=jnp.float32)
    mode_image, force_vector = element_contributions(basis_matrix, displacement, element_stiffening)
    weighted_image = (weights[:, None, None] * mode_image).astype(jnp.bfloat16)
    weighted_force = (force_vector * weights[None, :]).astype(jnp.bfloat16)
    tangent = lax.dot_general(
        basis_matrix,
        weighted_image,
        (((0, 1), (0, 1)), ((), ())),
        preferred_element_type=jnp.float32,
    )
    force_all = lax.dot_general(
        basis_matrix,
        weighted_force,
        (((0, 1), (1, 0)), ((), ())),
        preferred_element_type=jnp.float32,
    )
    halfway, force_part = (
        lax.psum_scatter(tangent, "blk", scatter_dimension=1, tiled=True),
        lax.psum_scatter(force_all, "blk", scatter_dimension=0, tiled=True),
    )
    mine = lax.psum_scatter(halfway, "elem", scatter_dimension=0, tiled=True)
    force_cols = lax.psum(force_part, "elem")
    scale = lax.rsqrt(24.0 * jnp.sum(set_size).astype(jnp.float32))
    return (mine * scale, force_cols * scale - load)


def signs(corner):
    return [1.0 if corner >> axis & 1 else -1.0 for axis in range(3)]


def signed_sum(terms, sign):
    total = terms[0] if sign[0] > 0 else -terms[0]
    for term, one in zip(terms[1:], sign[1:]):
        total = total + term if one > 0 else total - term
    return total


def fused_kernel(
    devs,
    basis_hbm,
    send_hbm,
    slot_hbm,
    size_hbm,
    weight_hbm,
    stiff_hbm,
    state_hbm,
    load_hbm,
    tangent_ref,
    residual_ref,
    basis_ref,
    send_ref,
    slot_ref,
    size_ref,
    weight_ref,
    stiff_ref,
    state_ref,
    load_ref,
    out_rows,
    arr,
    disp_out,
    disp_in,
    vt_ref,
    w_ref,
    part,
    recv_core,
    mid,
    recv_first,
    recv_second,
    acc,
    recv_z,
    in_sem,
    gather_send,
    gather_recv,
    disp_send,
    disp_recv,
    core_send,
    core_recv,
    first_send,
    first_recv,
    second_send,
    second_recv,
    z_send,
    z_recv,
):
    nodes = basis_ref.shape[1]
    modes = basis_ref.shape[2]
    slots = arr.shape[1]
    cap = slots // devs
    elements = weight_ref.shape[1]
    corners = 8 * elements
    planes = devs // 2
    rows = modes // devs
    chunks = modes // LANES
    f32, b16 = jnp.float32, jnp.bfloat16
    me = lax.axis_index("elem")
    blk = lax.axis_index("blk")
    x, z = lax.rem(me, 2), me // 2
    core, y = lax.rem(blk, 2), blk // 2
    core_peer = (me, y * 2 + 1 - core)
    y_peer = (me, (1 - y) * 2 + core)
    x_peer = (z * 2 + 1 - x, blk)

    def flipped(mask):
        dest, bit = 0, 1
        while bit < devs:
            low = lax.rem(me // bit, 2)
            dest = dest + bit * (1 - low if mask & bit else low)
            bit *= 2
        return dest

    def remote(src, dst, send, recv, peer):
        copy = pltpu.make_async_remote_copy(
            src_ref=src,
            dst_ref=dst,
            send_sem=send,
            recv_sem=recv,
            device_id=peer,
            device_id_type=MESH,
        )
        copy.start()
        return copy

    def by_lanes(q):
        return pl.ds(q * LANES, LANES)

    loads = []
    for i, (src, dst) in enumerate(
        (
            (send_hbm, send_ref),
            *(
                (basis_hbm.at[:, :, by_lanes(q)], basis_ref.at[:, :, by_lanes(q)])
                for q in range(chunks)
            ),
            (state_hbm, state_ref),
            (slot_hbm, slot_ref),
            (size_hbm, size_ref),
            (weight_hbm, weight_ref),
            (stiff_hbm, stiff_ref),
            (load_hbm, load_ref),
        )
    ):
        copy = pltpu.make_async_copy(src, dst, in_sem.at[i])
        copy.start()
        loads.append(copy)

    barrier = pltpu.get_barrier_semaphore()
    for step in range(1, devs):
        pl.semaphore_signal(
            barrier, inc=1, device_id=(lax.rem(me + step, devs), blk), device_id_type=MESH
        )
    for peer in (core_peer, y_peer):
        pl.semaphore_signal(barrier, inc=1, device_id=peer, device_id_type=MESH)

    loads[0].wait()
    asked = jnp.broadcast_to(send_ref[...], (nodes, slots))
    pick_t = jnp.where(lax.broadcasted_iota(jnp.int32, (nodes, slots), 0) == asked, 1.0, 0.0)
    pick = jnp.transpose(pick_t).astype(b16)
    mine = pl.ds(pl.multiple_of(me * cap, cap), cap)
    masks = list(range(devs - 1, 0, -1))
    gathers = [[] for _ in range(chunks)]

    def choose(q):
        loads[1 + q].wait()
        lanes = by_lanes(q)
        for c in range(3):
            out_rows[q, :, c * LANES : (c + 1) * LANES] = jnp.dot(
                pick, basis_ref[c, :, lanes], preferred_element_type=f32
            ).astype(b16)

    def send(q):
        for mask in masks:
            dest = flipped(mask)
            theirs = pl.ds(pl.multiple_of(dest * cap, cap), cap)
            gathers[q].append(
                remote(
                    out_rows.at[q, theirs, :],
                    arr.at[q, mine, :],
                    gather_send.at[q, mask - 1],
                    gather_recv.at[q, mask - 1],
                    (dest, blk),
                )
            )
        arr[q, mine, :] = out_rows[q, mine, :]

    choose(0)
    pl.semaphore_wait(barrier, devs + 1)
    send(0)
    for q in range(1, chunks):
        choose(q)

    loads[1 + chunks].wait()
    state = jnp.broadcast_to(state_ref[...].astype(f32).reshape(1, modes), (8, modes))
    component = lax.broadcasted_iota(jnp.int32, (8, modes), 0)
    moved = jnp.zeros((8, slots), f32)
    for c in range(3):
        state_c = jnp.where(component == c, state, 0.0).astype(b16)
        for q in range(chunks):
            moved = moved + lax.dot_general(
                state_c[:, q * LANES : (q + 1) * LANES],
                out_rows[q, :, c * LANES : (c + 1) * LANES],
                (((1,), (1,)), ((), ())),
                preferred_element_type=f32,
            )
    for tile in range(slots // LANES):
        disp_out[tile] = moved[:, tile * LANES : (tile + 1) * LANES]
    disps = []
    for mask in masks:
        dest = flipped(mask)
        disps.append(
            remote(
                disp_out.at[dest * cap // LANES],
                disp_in.at[me],
                disp_send.at[mask - 1],
                disp_recv.at[mask - 1],
                (dest, blk),
            )
        )
    disp_in[me] = disp_out[me * cap // LANES]
    for q in range(1, chunks):
        send(q)

    for copy in loads[2 + chunks :]:
        copy.wait()
    slot_row = jnp.concatenate([slot_ref[a : a + 1, :] for a in range(8)], axis=1)
    wanted = jnp.broadcast_to(slot_row, (slots, corners))
    spread_t = jnp.where(lax.broadcasted_iota(jnp.int32, (slots, corners), 0) == wanted, 1.0, 0.0)
    spread = jnp.transpose(spread_t)
    spread_t = spread_t.astype(b16)
    by_corner = [spread[a * elements : (a + 1) * elements] for a in range(8)]
    coef = jnp.concatenate(
        [0.25 * signed_sum(by_corner, [signs(a)[k] for a in range(8)]) for k in range(3)], axis=0
    ).astype(b16)
    spread = spread.astype(b16)
    lane_row = slot_row + lax.div(slot_row, cap) * (LANES - cap) + lax.rem(me * cap, LANES)
    wide = (devs * LANES, corners)
    spread_disp = jnp.where(
        lax.broadcasted_iota(jnp.int32, wide, 0) == jnp.broadcast_to(lane_row, wide), 1.0, 0.0
    ).astype(b16)

    for copy in disps:
        copy.wait_recv()
    whole = jnp.concatenate([disp_in[j] for j in range(devs)], axis=1)
    high = whole.astype(b16).astype(f32)
    middle = (whole - high).astype(b16).astype(f32)
    low = whole - high - middle
    pieces = jnp.dot(
        jnp.concatenate([high, middle, low], axis=0).astype(b16),
        spread_disp,
        preferred_element_type=f32,
    )
    picked = pieces[:8] + pieces[8:16] + pieces[16:24]
    disp = [
        [picked[c : c + 1, a * elements : (a + 1) * elements] for a in range(8)] for c in range(3)
    ]
    hgrad = [
        [0.25 * signed_sum(disp[c], [signs(a)[k] for a in range(8)]) for c in range(3)]
        for k in range(3)
    ]
    position = blk * elements + lax.broadcasted_iota(jnp.int32, (1, elements), 1)
    omega = jnp.where(position < size_ref[me], weight_ref[...], 0.0)
    volume = hgrad[0][0] + hgrad[1][1] + hgrad[2][2]
    square = stiff_ref[...] * volume * volume
    lam = 1.0 + square - 2.0 / 3.0
    press = volume + square * volume / 3.0 - 2.0 / 3.0 * volume
    wforce = []
    for c in range(3):
        stress = [
            hgrad[k][c] + hgrad[c][k] + press if k == c else hgrad[k][c] + hgrad[c][k]
            for k in range(3)
        ]
        row = jnp.concatenate(
            [0.25 * omega * (signed_sum(stress, signs(a)) + disp[c][a]) for a in range(8)], axis=1
        )
        wforce.append(jnp.broadcast_to(row, (8, corners)).astype(b16))
    both = jnp.concatenate([0.25 * omega, lam], axis=1)
    columns = jnp.transpose(jnp.broadcast_to(both, (LANES, 2 * elements)))
    quarter, lam = columns[:elements], columns[elements:]

    def place(i, j, block, tail):
        to_y, to_core = j // 2, j % 2
        for to_x in range(2):
            f, s = (to_y, to_x) if i % 2 == 0 else (to_x, to_y)
            part[i, to_core, f, s, :rows] = block[to_x * rows : (to_x + 1) * rows]
            part[i, to_core, f, s, rows:] = tail

    def half_of(ref, i, to_y):
        return ref.at[to_y] if i % 2 == 0 else ref.at[:, to_y]

    def to_other_core(q, which):
        for i in which:
            for to_y in range(2):
                if max(i, 2 * to_y + 1) == q:
                    cores[i].append(
                        remote(
                            half_of(part.at[i, 1 - core], i, to_y),
                            half_of(recv_core.at[i], i, to_y),
                            core_send.at[i, to_y],
                            core_recv.at[i, to_y],
                            core_peer,
                        )
                    )

    tails = []
    cores = [[] for _ in range(planes)]
    for q in range(chunks):
        lanes = pl.ds(q * LANES, LANES)
        for copy in gathers[q]:
            copy.wait_recv()
        arrived = arr[q]
        vt = lax.dot_general(
            arrived, spread_t, (((0,), (0,)), ((), ())), preferred_element_type=f32
        ).astype(b16)
        v = jnp.dot(spread, arrived, preferred_element_type=f32)
        g = jnp.dot(coef, arrived, preferred_element_type=f32)
        grad = [
            [
                g[k * elements : (k + 1) * elements, c * LANES : (c + 1) * LANES]
                for c in range(3)
            ]
            for k in range(3)
        ]
        trace = lam * (grad[0][0] + grad[1][1] + grad[2][2])
        tail = jnp.zeros((8, LANES), f32)
        for c in range(3):
            vt_ref[c, lanes, :] = vt[c * LANES : (c + 1) * LANES]
            v_c = v[:, c * LANES : (c + 1) * LANES]
            terms = [
                grad[k][c] + grad[c][k] + trace if k == c else grad[k][c] + grad[c][k]
                for k in range(3)
            ]
            for a in range(4):
                half = signed_sum(terms, signs(a))
                for corner, image in ((a, half), (7 - a, -half)):
                    at = corner * elements
                    w_ref[c, pl.ds(at, elements), lanes] = (
                        quarter * (image + v_c[at : at + elements])
                    ).astype(b16)
            tail = tail + jnp.dot(wforce[c], v_c.astype(b16), preferred_element_type=f32)
        tails.append(tail)
        down = sum(
            jnp.dot(
                vt_ref[c, : (q + 1) * LANES, :], w_ref[c, :, lanes], preferred_element_type=f32
            )
            for c in range(3)
        )
        for i in range(q + 1):
            place(i, q, down[i * LANES : (i + 1) * LANES], tail)
        to_other_core(q, range(q))
        if q > 0:
            across = sum(
                jnp.dot(
                    vt_ref[c, lanes, :], w_ref[c, :, : q * LANES], preferred_element_type=f32
                )
                for c in range(3)
            )
            for j in range(q):
                place(q, j, across[:, j * LANES : (j + 1) * LANES], tails[j])
            to_other_core(q, (q,))

    firsts, seconds = [], []
    order = (((y, y_peer), (x, x_peer)), ((x, x_peer), (y, y_peer)))
    for i in range(planes):
        at, peer = order[i % 2][0]
        for copy in cores[i]:
            copy.wait_recv()
        mid[i, 1 - at] = part[i, core, 1 - at] + recv_core[i, 1 - at]
        firsts.append(
            remote(mid.at[i, 1 - at], recv_first.at[i], first_send.at[i], first_recv.at[i], peer)
        )
    for i in range(planes):
        at = order[i % 2][0][0]
        there, peer = order[i % 2][1]
        mid[i, at] = part[i, core, at] + recv_core[i, at]
        firsts[i].wait_recv()
        mid[i, at, 1 - there] = mid[i, at, 1 - there] + recv_first[i, 1 - there]
        seconds.append(
            remote(
                mid.at[i, at, 1 - there],
                recv_second.at[i],
                second_send.at[i],
                second_recv.at[i],
                peer,
            )
        )

    def z_copy(i):
        slot = lax.rem(z - i + planes - 1, planes)
        return pltpu.make_async_remote_copy(
            src_ref=acc.at[i],
            dst_ref=recv_z.at[slot],
            send_sem=z_send.at[i],
            recv_sem=z_recv.at[slot],
            device_id=(i * 2 + x, blk),
            device_id_type=MESH,
        )

    for i in range(planes):
        at = order[i % 2][0][0]
        there = order[i % 2][1][0]
        seconds[i].wait_recv()
        acc[i] = mid[i, at, there] + recv_first[i, there] + recv_second[i]

        @pl.when(z != i)
        def _(i=i):
            z_copy(i).start()

    count = size_ref[0]
    for i in range(1, devs):
        count = count + size_ref[i]
    scale = lax.rsqrt(jnp.full((8, LANES), 24.0 * count.astype(f32), f32))
    total = acc[z]
    for slot in range(planes - 1):
        pltpu.make_async_remote_copy(
            src_ref=acc.at[slot],
            dst_ref=recv_z.at[slot],
            send_sem=z_send.at[slot],
            recv_sem=z_recv.at[slot],
            device_id=x_peer,
            device_id_type=MESH,
        ).wait_recv()
        total = total + recv_z[slot]
    tangent_ref[...] = total[:rows] * jnp.tile(scale, (rows // 8, 1))
    residual_ref[...] = (total[rows:] * scale)[:1] - load_ref[...]
    for copy in sum(gathers, []) + disps + sum(cores, []) + firsts + seconds:
        copy.wait_send()
    for i in range(planes):

        @pl.when(z != i)
        def _(i=i):
            z_copy(i).wait_send()


def hand_on(tangent_ref, residual_ref, tangent_out, residual_out, sem):
    copies = [
        pltpu.make_async_copy(tangent_ref, tangent_out, sem.at[0]),
        pltpu.make_async_copy(residual_ref, residual_out, sem.at[1]),
    ]
    for copy in copies:
        copy.start()
    for copy in copies:
        copy.wait()


def fused(devs, basis, send_rows, elem_slot, set_size, elem_weight, element_stiffening, state, load):
    nodes, _, modes = basis.shape
    slots = send_rows.shape[2]
    elements = elem_slot.shape[1]
    corners = 8 * elements
    rows = modes // devs
    planes = devs // 2
    chunks = modes // LANES
    block = (rows + 8, LANES)
    f32, b16 = jnp.float32, jnp.bfloat16
    dma = pltpu.SemaphoreType.DMA
    vmem = pl.BlockSpec(memory_space=pltpu.VMEM)
    anywhere = pl.BlockSpec(memory_space=pl.ANY)
    tangent, residual = pl.pallas_call(
        functools.partial(fused_kernel, devs),
        out_shape=(
            jax.ShapeDtypeStruct((rows, LANES), f32),
            jax.ShapeDtypeStruct((1, LANES), f32),
        ),
        in_specs=[anywhere] * 8,
        out_specs=(vmem, vmem),
        scratch_shapes=[
            pltpu.VMEM((3, nodes, modes), b16),
            pltpu.VMEM((1, slots), jnp.int32),
            pltpu.VMEM((8, elements), jnp.int32),
            pltpu.SMEM(set_size.shape, jnp.int32),
            pltpu.VMEM((1, elements), f32),
            pltpu.VMEM((1, elements), f32),
            pltpu.VMEM((modes,), b16),
            pltpu.VMEM((1, LANES), f32),
            pltpu.VMEM((chunks, slots, 3 * LANES), b16),
            pltpu.VMEM((chunks, slots, 3 * LANES), b16),
            pltpu.VMEM((slots // LANES, 8, LANES), f32),
            pltpu.VMEM((devs, 8, LANES), f32),
            pltpu.VMEM((3, modes, corners), b16),
            pltpu.VMEM((3, corners, modes), b16),
            pltpu.VMEM((planes, 2, 2, 2) + block, f32),
            pltpu.VMEM((planes, 2, 2) + block, f32),
            pltpu.VMEM((planes, 2, 2) + block, f32),
            pltpu.VMEM((planes, 2) + block, f32),
            pltpu.VMEM((planes,) + block, f32),
            pltpu.VMEM((planes,) + block, f32),
            pltpu.VMEM((planes - 1,) + block, f32),
            dma((7 + chunks,)),
            dma((chunks, devs - 1)),
            dma((chunks, devs - 1)),
            dma((devs - 1,)),
            dma((devs - 1,)),
            dma((planes, 2)),
            dma((planes, 2)),
            dma((planes,)),
            dma((planes,)),
            dma((planes,)),
            dma((planes,)),
            dma((planes,)),
            dma((planes - 1,)),
        ],
        compiler_params=pltpu.CompilerParams(
            collective_id=0, has_side_effects=True, vmem_limit_bytes=60 * 1024 * 1024
        ),
        cost_estimate=pl.CostEstimate(
            flops=6 * modes * modes * corners, bytes_accessed=2 * basis.size, transcendentals=0
        ),
        name="galerkin",
    )(
        jnp.transpose(basis, (1, 0, 2)),
        send_rows.reshape(1, slots),
        elem_slot,
        set_size,
        elem_weight.reshape(1, elements),
        element_stiffening.reshape(1, elements),
        state,
        load.reshape(1, LANES),
    )
    tangent, residual = pl.pallas_call(
        hand_on,
        out_shape=(
            jax.ShapeDtypeStruct(tangent.shape, f32),
            jax.ShapeDtypeStruct(residual.shape, f32),
        ),
        in_specs=[anywhere] * 2,
        out_specs=(anywhere, anywhere),
        scratch_shapes=[dma((2,))],
        compiler_params=pltpu.CompilerParams(vmem_limit_bytes=60 * 1024 * 1024),
        name="hand_on",
    )(tangent, residual)
    return tangent, residual.reshape(LANES)


def solution(mesh):
    in_specs = (
        P("elem", None, None),
        P("elem", "blk", None),
        P(None, ("elem", "blk")),
        P(),
        P(("elem", "blk")),
        P(("elem", "blk")),
        P(),
        P("blk"),
    )
    out_specs = (P("elem", "blk"), P("blk"))
    devs, blocks = mesh.shape["elem"], mesh.shape["blk"]

    def run(*args):
        modes, slots, elements = args[0].shape[2], args[1].shape[2], args[2].shape[1] // mesh.size
        fits = (
            blocks == 4
            and modes == blocks * LANES
            and devs == 2 * blocks
            and modes % (8 * devs) == 0
            and slots % (16 * devs) == 0
            and 2 * elements == LANES
            and slots % LANES == 0
            and LANES % (slots // devs) == 0
        )
        part = functools.partial(fused, devs) if fits else local
        return jax.shard_map(
            part, mesh=mesh, in_specs=in_specs, out_specs=out_specs, check_vma=False
        )(*args)

    return run
```

```python
import functools

import jax
import jax.numpy as jnp
from jax import lax
from jax.experimental import pallas as pl
from jax.experimental.pallas import tpu as pltpu
from jax.sharding import PartitionSpec as P

LANES = 128
MESH = pl.DeviceIdType.MESH


def corner_grads():
    corner = jnp.arange(8)[:, None]
    bit = corner // 2 ** jnp.arange(3)[None, :] % 2
    return (bit * 2 - 1).astype(jnp.float32) * 0.25


def element_contributions(basis_matrix, displacement, stiffening_power):
    grads = corner_grads()
    element_count = basis_matrix.shape[0]
    basis_modes = basis_matrix.shape[2]
    corner_nodes = basis_matrix.reshape(element_count, 8, 3, basis_modes)
    grad_basis = jnp.einsum(
        "ak,eacm->ekcm",
        grads.astype(jnp.bfloat16),
        corner_nodes,
        preferred_element_type=jnp.float32,
    )
    moved = displacement.reshape(8, 3, element_count)
    hgrad = jnp.einsum("ak,ace->kce", grads, moved, precision=lax.Precision.HIGHEST)
    volume = hgrad[0, 0] + hgrad[1, 1] + hgrad[2, 2]
    stiff = 1.0 + stiffening_power * volume**2 - 2.0 / 3.0
    press = volume + stiffening_power * volume**3 / 3.0 - 2.0 / 3.0 * volume
    eye = jnp.eye(3, dtype=jnp.float32)
    stress = hgrad + jnp.transpose(hgrad, (1, 0, 2)) + press[None, None, :] * eye[:, :, None]
    force_vector = (
        jnp.einsum("ak,kce->ace", grads, stress, precision=lax.Precision.HIGHEST).reshape(
            24, element_count
        )
        + 0.25 * displacement
    )
    sym = grad_basis + jnp.transpose(grad_basis, (0, 2, 1, 3))
    trace_basis = grad_basis[:, 0, 0] + grad_basis[:, 1, 1] + grad_basis[:, 2, 2]
    mode_image = jnp.einsum("ak,ekcm->eacm", grads, sym, precision=lax.Precision.HIGHEST)
    mode_image = (
        mode_image
        + stiff[:, None, None, None] * grads[None, :, :, None] * trace_basis[:, None, None, :]
        + 0.25 * corner_nodes.astype(jnp.float32)
    )
    return (mode_image.reshape(element_count, 24, basis_modes), force_vector)


def local(basis, send_rows, elem_slot, set_size, elem_weight, element_stiffening, state, load):
    nodes = basis.shape[0]
    basis_modes = basis.shape[2]
    flat = basis.reshape(nodes, 3 * basis_modes)
    outgoing = jnp.take(flat, send_rows[0, 0], axis=0)
    arrived = lax.all_to_all(outgoing, "elem", split_axis=0, concat_axis=0, tiled=True)
    element_count = elem_slot.shape[1]
    chosen_elements = jnp.take(arrived, elem_slot.T.reshape(-1), axis=0)
    basis_matrix = chosen_elements.reshape(element_count, 24, basis_modes)
    set_index = lax.axis_index("elem")
    block_index = lax.axis_index("blk")
    live = lax.dynamic_index_in_dim(set_size, set_index, keepdims=False)
    position = block_index * element_count + jnp.arange(element_count, dtype=jnp.int32)
    weights = jnp.where(position < live, elem_weight, jnp.zeros_like(elem_weight))
    displacement = jnp.einsum("agd,d->ga", basis_matrix, state, preferred_element_type=jnp.float32)
    mode_image, force_vector = element_contributions(basis_matrix, displacement, element_stiffening)
    weighted_image = (weights[:, None, None] * mode_image).astype(jnp.bfloat16)
    weighted_force = (force_vector * weights[None, :]).astype(jnp.bfloat16)
    tangent = lax.dot_general(
        basis_matrix,
        weighted_image,
        (((0, 1), (0, 1)), ((), ())),
        preferred_element_type=jnp.float32,
    )
    force_all = lax.dot_general(
        basis_matrix,
        weighted_force,
        (((0, 1), (1, 0)), ((), ())),
        preferred_element_type=jnp.float32,
    )
    halfway, force_part = (
        lax.psum_scatter(tangent, "blk", scatter_dimension=1, tiled=True),
        lax.psum_scatter(force_all, "blk", scatter_dimension=0, tiled=True),
    )
    mine = lax.psum_scatter(halfway, "elem", scatter_dimension=0, tiled=True)
    force_cols = lax.psum(force_part, "elem")
    scale = lax.rsqrt(24.0 * jnp.sum(set_size).astype(jnp.float32))
    return (mine * scale, force_cols * scale - load)


def signs(corner):
    return [1.0 if corner >> axis & 1 else -1.0 for axis in range(3)]


def signed_sum(terms, sign):
    total = terms[0] if sign[0] > 0 else -terms[0]
    for term, one in zip(terms[1:], sign[1:]):
        total = total + term if one > 0 else total - term
    return total


def fused_kernel(
    devs,
    basis_hbm,
    send_hbm,
    slot_hbm,
    size_hbm,
    weight_hbm,
    stiff_hbm,
    state_hbm,
    load_hbm,
    tangent_ref,
    residual_ref,
    basis_ref,
    send_ref,
    slot_ref,
    size_ref,
    weight_ref,
    stiff_ref,
    state_ref,
    load_ref,
    out_rows,
    arr,
    disp_out,
    disp_in,
    vt_ref,
    w_ref,
    part,
    recv_core,
    mid,
    recv_first,
    recv_second,
    acc,
    recv_z,
    in_sem,
    gather_send,
    gather_recv,
    disp_send,
    disp_recv,
    core_send,
    core_recv,
    first_send,
    first_recv,
    second_send,
    second_recv,
    z_send,
    z_recv,
):
    nodes = basis_ref.shape[1]
    modes = basis_ref.shape[2]
    slots = arr.shape[1]
    cap = slots // devs
    elements = weight_ref.shape[1]
    corners = 8 * elements
    planes = devs // 2
    rows = modes // devs
    chunks = modes // LANES
    f32, b16 = jnp.float32, jnp.bfloat16
    me = lax.axis_index("elem")
    blk = lax.axis_index("blk")
    x, z = lax.rem(me, 2), me // 2
    core, y = lax.rem(blk, 2), blk // 2
    core_peer = (me, y * 2 + 1 - core)
    y_peer = (me, (1 - y) * 2 + core)
    x_peer = (z * 2 + 1 - x, blk)

    def flipped(mask):
        dest, bit = 0, 1
        while bit < devs:
            low = lax.rem(me // bit, 2)
            dest = dest + bit * (1 - low if mask & bit else low)
            bit *= 2
        return dest

    def remote(src, dst, send, recv, peer):
        copy = pltpu.make_async_remote_copy(
            src_ref=src,
            dst_ref=dst,
            send_sem=send,
            recv_sem=recv,
            device_id=peer,
            device_id_type=MESH,
        )
        copy.start()
        return copy

    loads = []
    for i, (src, dst) in enumerate(
        (
            (send_hbm, send_ref),
            (basis_hbm, basis_ref),
            (state_hbm, state_ref),
            (slot_hbm, slot_ref),
            (size_hbm, size_ref),
            (weight_hbm, weight_ref),
            (stiff_hbm, stiff_ref),
            (load_hbm, load_ref),
        )
    ):
        copy = pltpu.make_async_copy(src, dst, in_sem.at[i])
        copy.start()
        loads.append(copy)

    barrier = pltpu.get_barrier_semaphore()
    for step in range(1, devs):
        pl.semaphore_signal(
            barrier, inc=1, device_id=(lax.rem(me + step, devs), blk), device_id_type=MESH
        )
    for peer in (core_peer, y_peer):
        pl.semaphore_signal(barrier, inc=1, device_id=peer, device_id_type=MESH)

    loads[0].wait()
    asked = jnp.broadcast_to(send_ref[...], (nodes, slots))
    pick_t = jnp.where(lax.broadcasted_iota(jnp.int32, (nodes, slots), 0) == asked, 1.0, 0.0)
    pick = jnp.transpose(pick_t).astype(b16)
    mine = pl.ds(pl.multiple_of(me * cap, cap), cap)
    masks = list(range(devs - 1, 0, -1))
    gathers = [[] for _ in range(chunks)]

    def choose(q):
        lanes = pl.ds(q * LANES, LANES)
        for c in range(3):
            out_rows[q, :, c * LANES : (c + 1) * LANES] = jnp.dot(
                pick, basis_ref[c, :, lanes], preferred_element_type=f32
            ).astype(b16)

    def send(q):
        for mask in masks:
            dest = flipped(mask)
            theirs = pl.ds(pl.multiple_of(dest * cap, cap), cap)
            gathers[q].append(
                remote(
                    out_rows.at[q, theirs, :],
                    arr.at[q, mine, :],
                    gather_send.at[q, mask - 1],
                    gather_recv.at[q, mask - 1],
                    (dest, blk),
                )
            )
        arr[q, mine, :] = out_rows[q, mine, :]

    loads[1].wait()
    choose(0)
    pl.semaphore_wait(barrier, devs + 1)
    send(0)
    for q in range(1, chunks):
        choose(q)

    loads[2].wait()
    state = jnp.broadcast_to(state_ref[...].astype(f32).reshape(1, modes), (8, modes))
    component = lax.broadcasted_iota(jnp.int32, (8, modes), 0)
    moved = jnp.zeros((8, slots), f32)
    for c in range(3):
        state_c = jnp.where(component == c, state, 0.0).astype(b16)
        for q in range(chunks):
            moved = moved + lax.dot_general(
                state_c[:, q * LANES : (q + 1) * LANES],
                out_rows[q, :, c * LANES : (c + 1) * LANES],
                (((1,), (1,)), ((), ())),
                preferred_element_type=f32,
            )
    for tile in range(slots // LANES):
        disp_out[tile] = moved[:, tile * LANES : (tile + 1) * LANES]
    disps = []
    for mask in masks:
        dest = flipped(mask)
        disps.append(
            remote(
                disp_out.at[dest * cap // LANES],
                disp_in.at[me],
                disp_send.at[mask - 1],
                disp_recv.at[mask - 1],
                (dest, blk),
            )
        )
    disp_in[me] = disp_out[me * cap // LANES]
    for q in range(1, chunks):
        send(q)

    for copy in loads[3:]:
        copy.wait()
    slot_row = jnp.concatenate([slot_ref[a : a + 1, :] for a in range(8)], axis=1)
    wanted = jnp.broadcast_to(slot_row, (slots, corners))
    spread_t = jnp.where(lax.broadcasted_iota(jnp.int32, (slots, corners), 0) == wanted, 1.0, 0.0)
    spread = jnp.transpose(spread_t)
    spread_t = spread_t.astype(b16)
    by_corner = [spread[a * elements : (a + 1) * elements] for a in range(8)]
    coef = jnp.concatenate(
        [0.25 * signed_sum(by_corner, [signs(a)[k] for a in range(8)]) for k in range(3)], axis=0
    ).astype(b16)
    spread = spread.astype(b16)
    lane_row = slot_row + lax.div(slot_row, cap) * (LANES - cap) + lax.rem(me * cap, LANES)
    wide = (devs * LANES, corners)
    spread_disp = jnp.where(
        lax.broadcasted_iota(jnp.int32, wide, 0) == jnp.broadcast_to(lane_row, wide), 1.0, 0.0
    ).astype(b16)

    for copy in disps:
        copy.wait_recv()
    whole = jnp.concatenate([disp_in[j] for j in range(devs)], axis=1)
    high = whole.astype(b16).astype(f32)
    middle = (whole - high).astype(b16).astype(f32)
    low = whole - high - middle
    pieces = jnp.dot(
        jnp.concatenate([high, middle, low], axis=0).astype(b16),
        spread_disp,
        preferred_element_type=f32,
    )
    picked = pieces[:8] + pieces[8:16] + pieces[16:24]
    disp = [
        [picked[c : c + 1, a * elements : (a + 1) * elements] for a in range(8)] for c in range(3)
    ]
    hgrad = [
        [0.25 * signed_sum(disp[c], [signs(a)[k] for a in range(8)]) for c in range(3)]
        for k in range(3)
    ]
    position = blk * elements + lax.broadcasted_iota(jnp.int32, (1, elements), 1)
    omega = jnp.where(position < size_ref[me], weight_ref[...], 0.0)
    volume = hgrad[0][0] + hgrad[1][1] + hgrad[2][2]
    square = stiff_ref[...] * volume * volume
    lam = 1.0 + square - 2.0 / 3.0
    press = volume + square * volume / 3.0 - 2.0 / 3.0 * volume
    wforce = []
    for c in range(3):
        stress = [
            hgrad[k][c] + hgrad[c][k] + press if k == c else hgrad[k][c] + hgrad[c][k]
            for k in range(3)
        ]
        row = jnp.concatenate(
            [0.25 * omega * (signed_sum(stress, signs(a)) + disp[c][a]) for a in range(8)], axis=1
        )
        wforce.append(jnp.broadcast_to(row, (8, corners)).astype(b16))
    both = jnp.concatenate([0.25 * omega, lam], axis=1)
    columns = jnp.transpose(jnp.broadcast_to(both, (LANES, 2 * elements)))
    quarter, lam = columns[:elements], columns[elements:]

    def place(i, j, block, tail):
        to_y, to_core = j // 2, j % 2
        for to_x in range(2):
            f, s = (to_y, to_x) if i % 2 == 0 else (to_x, to_y)
            part[i, to_core, f, s, :rows] = block[to_x * rows : (to_x + 1) * rows]
            part[i, to_core, f, s, rows:] = tail

    def half_of(ref, i, to_y):
        return ref.at[to_y] if i % 2 == 0 else ref.at[:, to_y]

    tails = []
    cores = [[] for _ in range(planes)]
    for q in range(chunks):
        lanes = pl.ds(q * LANES, LANES)
        for copy in gathers[q]:
            copy.wait_recv()
        arrived = arr[q]
        vt = lax.dot_general(
            arrived, spread_t, (((0,), (0,)), ((), ())), preferred_element_type=f32
        ).astype(b16)
        v = jnp.dot(spread, arrived, preferred_element_type=f32)
        g = jnp.dot(coef, arrived, preferred_element_type=f32)
        grad = [
            [
                g[k * elements : (k + 1) * elements, c * LANES : (c + 1) * LANES]
                for c in range(3)
            ]
            for k in range(3)
        ]
        trace = lam * (grad[0][0] + grad[1][1] + grad[2][2])
        tail = jnp.zeros((8, LANES), f32)
        for c in range(3):
            vt_ref[c, lanes, :] = vt[c * LANES : (c + 1) * LANES]
            v_c = v[:, c * LANES : (c + 1) * LANES]
            terms = [
                grad[k][c] + grad[c][k] + trace if k == c else grad[k][c] + grad[c][k]
                for k in range(3)
            ]
            for a in range(4):
                half = signed_sum(terms, signs(a))
                for corner, image in ((a, half), (7 - a, -half)):
                    at = corner * elements
                    w_ref[c, pl.ds(at, elements), lanes] = (
                        quarter * (image + v_c[at : at + elements])
                    ).astype(b16)
            tail = tail + jnp.dot(wforce[c], v_c.astype(b16), preferred_element_type=f32)
        tails.append(tail)
        down = sum(
            jnp.dot(
                vt_ref[c, : (q + 1) * LANES, :], w_ref[c, :, lanes], preferred_element_type=f32
            )
            for c in range(3)
        )
        for i in range(q + 1):
            place(i, q, down[i * LANES : (i + 1) * LANES], tail)
        if q > 0:
            across = sum(
                jnp.dot(
                    vt_ref[c, lanes, :], w_ref[c, :, : q * LANES], preferred_element_type=f32
                )
                for c in range(3)
            )
            for j in range(q):
                place(q, j, across[:, j * LANES : (j + 1) * LANES], tails[j])
        for i in range(planes):
            for to_y in range(2):
                if max(i, 2 * to_y + 1) == q:
                    cores[i].append(
                        remote(
                            half_of(part.at[i, 1 - core], i, to_y),
                            half_of(recv_core.at[i], i, to_y),
                            core_send.at[i, to_y],
                            core_recv.at[i, to_y],
                            core_peer,
                        )
                    )

    firsts, seconds = [], []
    order = (((y, y_peer), (x, x_peer)), ((x, x_peer), (y, y_peer)))
    for i in range(planes):
        at, peer = order[i % 2][0]
        for copy in cores[i]:
            copy.wait_recv()
        mid[i, 1 - at] = part[i, core, 1 - at] + recv_core[i, 1 - at]
        firsts.append(
            remote(mid.at[i, 1 - at], recv_first.at[i], first_send.at[i], first_recv.at[i], peer)
        )
    for i in range(planes):
        at = order[i % 2][0][0]
        there, peer = order[i % 2][1]
        mid[i, at] = part[i, core, at] + recv_core[i, at]
        firsts[i].wait_recv()
        mid[i, at, 1 - there] = mid[i, at, 1 - there] + recv_first[i, 1 - there]
        seconds.append(
            remote(
                mid.at[i, at, 1 - there],
                recv_second.at[i],
                second_send.at[i],
                second_recv.at[i],
                peer,
            )
        )

    def z_copy(i):
        slot = lax.rem(z - i + planes - 1, planes)
        return pltpu.make_async_remote_copy(
            src_ref=acc.at[i],
            dst_ref=recv_z.at[slot],
            send_sem=z_send.at[i],
            recv_sem=z_recv.at[slot],
            device_id=(i * 2 + x, blk),
            device_id_type=MESH,
        )

    for i in range(planes):
        at = order[i % 2][0][0]
        there = order[i % 2][1][0]
        seconds[i].wait_recv()
        acc[i] = mid[i, at, there] + recv_first[i, there] + recv_second[i]

        @pl.when(z != i)
        def _(i=i):
            z_copy(i).start()

    count = size_ref[0]
    for i in range(1, devs):
        count = count + size_ref[i]
    scale = lax.rsqrt(jnp.full((8, LANES), 24.0 * count.astype(f32), f32))
    total = acc[z]
    for slot in range(planes - 1):
        pltpu.make_async_remote_copy(
            src_ref=acc.at[slot],
            dst_ref=recv_z.at[slot],
            send_sem=z_send.at[slot],
            recv_sem=z_recv.at[slot],
            device_id=x_peer,
            device_id_type=MESH,
        ).wait_recv()
        total = total + recv_z[slot]
    tangent_ref[...] = total[:rows] * jnp.tile(scale, (rows // 8, 1))
    residual_ref[...] = (total[rows:] * scale)[:1] - load_ref[...]
    for copy in sum(gathers, []) + disps + sum(cores, []) + firsts + seconds:
        copy.wait_send()
    for i in range(planes):

        @pl.when(z != i)
        def _(i=i):
            z_copy(i).wait_send()


def hand_on(tangent_ref, residual_ref, tangent_out, residual_out, sem):
    copies = [
        pltpu.make_async_copy(tangent_ref, tangent_out, sem.at[0]),
        pltpu.make_async_copy(residual_ref, residual_out, sem.at[1]),
    ]
    for copy in copies:
        copy.start()
    for copy in copies:
        copy.wait()


def fused(devs, basis, send_rows, elem_slot, set_size, elem_weight, element_stiffening, state, load):
    nodes, _, modes = basis.shape
    slots = send_rows.shape[2]
    elements = elem_slot.shape[1]
    corners = 8 * elements
    rows = modes // devs
    planes = devs // 2
    chunks = modes // LANES
    block = (rows + 8, LANES)
    f32, b16 = jnp.float32, jnp.bfloat16
    dma = pltpu.SemaphoreType.DMA
    vmem = pl.BlockSpec(memory_space=pltpu.VMEM)
    anywhere = pl.BlockSpec(memory_space=pl.ANY)
    tangent, residual = pl.pallas_call(
        functools.partial(fused_kernel, devs),
        out_shape=(
            jax.ShapeDtypeStruct((rows, LANES), f32),
            jax.ShapeDtypeStruct((1, LANES), f32),
        ),
        in_specs=[anywhere] * 8,
        out_specs=(vmem, vmem),
        scratch_shapes=[
            pltpu.VMEM((3, nodes, modes), b16),
            pltpu.VMEM((1, slots), jnp.int32),
            pltpu.VMEM((8, elements), jnp.int32),
            pltpu.SMEM(set_size.shape, jnp.int32),
            pltpu.VMEM((1, elements), f32),
            pltpu.VMEM((1, elements), f32),
            pltpu.VMEM((modes,), b16),
            pltpu.VMEM((1, LANES), f32),
            pltpu.VMEM((chunks, slots, 3 * LANES), b16),
            pltpu.VMEM((chunks, slots, 3 * LANES), b16),
            pltpu.VMEM((slots // LANES, 8, LANES), f32),
            pltpu.VMEM((devs, 8, LANES), f32),
            pltpu.VMEM((3, modes, corners), b16),
            pltpu.VMEM((3, corners, modes), b16),
            pltpu.VMEM((planes, 2, 2, 2) + block, f32),
            pltpu.VMEM((planes, 2, 2) + block, f32),
            pltpu.VMEM((planes, 2, 2) + block, f32),
            pltpu.VMEM((planes, 2) + block, f32),
            pltpu.VMEM((planes,) + block, f32),
            pltpu.VMEM((planes,) + block, f32),
            pltpu.VMEM((planes - 1,) + block, f32),
            dma((8,)),
            dma((chunks, devs - 1)),
            dma((chunks, devs - 1)),
            dma((devs - 1,)),
            dma((devs - 1,)),
            dma((planes, 2)),
            dma((planes, 2)),
            dma((planes,)),
            dma((planes,)),
            dma((planes,)),
            dma((planes,)),
            dma((planes,)),
            dma((planes - 1,)),
        ],
        compiler_params=pltpu.CompilerParams(
            collective_id=0, has_side_effects=True, vmem_limit_bytes=60 * 1024 * 1024
        ),
        cost_estimate=pl.CostEstimate(
            flops=6 * modes * modes * corners, bytes_accessed=2 * basis.size, transcendentals=0
        ),
        name="galerkin",
    )(
        jnp.transpose(basis, (1, 0, 2)),
        send_rows.reshape(1, slots),
        elem_slot,
        set_size,
        elem_weight.reshape(1, elements),
        element_stiffening.reshape(1, elements),
        state,
        load.reshape(1, LANES),
    )
    tangent, residual = pl.pallas_call(
        hand_on,
        out_shape=(
            jax.ShapeDtypeStruct(tangent.shape, f32),
            jax.ShapeDtypeStruct(residual.shape, f32),
        ),
        in_specs=[anywhere] * 2,
        out_specs=(anywhere, anywhere),
        scratch_shapes=[dma((2,))],
        compiler_params=pltpu.CompilerParams(vmem_limit_bytes=60 * 1024 * 1024),
        name="hand_on",
    )(tangent, residual)
    return tangent, residual.reshape(LANES)


def solution(mesh):
    in_specs = (
        P("elem", None, None),
        P("elem", "blk", None),
        P(None, ("elem", "blk")),
        P(),
        P(("elem", "blk")),
        P(("elem", "blk")),
        P(),
        P("blk"),
    )
    out_specs = (P("elem", "blk"), P("blk"))
    devs, blocks = mesh.shape["elem"], mesh.shape["blk"]

    def run(*args):
        modes, slots, elements = args[0].shape[2], args[1].shape[2], args[2].shape[1] // mesh.size
        fits = (
            blocks == 4
            and modes == blocks * LANES
            and devs == 2 * blocks
            and modes % (8 * devs) == 0
            and slots % (16 * devs) == 0
            and 2 * elements == LANES
            and slots % LANES == 0
            and LANES % (slots // devs) == 0
        )
        part = functools.partial(fused, devs) if fits else local
        return jax.shard_map(
            part, mesh=mesh, in_specs=in_specs, out_specs=out_specs, check_vma=False
        )(*args)

    return run
```
